32 devices in a mesh: parts: 2 (over y), col: 16 (over z, x, core).
Axes of the slice: x: 2, y: 2, z: 4, core: 2. Of those that a mesh axis runs over, the one named last changes fastest.
Arguments:
- counts: int32 [1024, 8192], P('parts', 'col'), parts along dimension 0, may hold values from 0 to 4095, as said below
- row_totals: int32 [1024], P('parts'), parts along dimension 0, may hold values from 1000 to 999999
- column_totals: int32 [16384], P(('parts', 'col')), parts along dimension 0, may hold values from 1000 to 999999
- row_master: float32 [1024, 256], P(('parts', 'col')), parts along dimension 0, may hold values from -1.5 to 1.5
- row_history: float32 [1024, 256], P(('parts', 'col')), parts along dimension 0, may hold values from 0.01 to 0.1
- column_master: float32 [16384, 256], P(('parts', 'col')), parts along dimension 0, may hold values from -1.5 to 1.5
- column_history: float32 [16384, 256], P(('parts', 'col')), parts along dimension 0, may hold values from 0.01 to 0.1
Outputs:
- grid_rows: bfloat16 [1024, 256], P('parts'), parts along dimension 0
- new_row_master: float32 [1024, 256], P(('parts', 'col')), parts along dimension 0
- new_row_history: float32 [1024, 256], P(('parts', 'col')), parts along dimension 0
- new_column_master: float32 [16384, 256], P(('parts', 'col')), parts along dimension 0
- new_column_history: float32 [16384, 256], P(('parts', 'col')), parts along dimension 0
The draws below stay inside these ranges and needn't reach their ends.
There are 2 independent parts, one for each index of `parts`. The reference program is written for one: setup_inputs(seed, part) draws one part's arguments, and reference() takes and returns one part's arrays. A program takes and returns all parts, laid end to end along the dimension named above; each array names one. Nothing has to cross between parts.
Inputs may be any that keep to these rules, and one draw needn't show every extreme that they name: Co-occurrence counts; some are zero, and their sizes spread over several powers of two.
All inputs are finite; a program needn't handle non-finite values.
Results may differ from the reference program's by a relative error of at most 0.0075.
Values may be sent and summed in bfloat16 or wider, within the bound.
No kernel may reach another device: no remote copies, remote signals or barrier semaphores. Data moves between devices by JAX's collectives and lax.ppermute only.
A program may use at most 64 MiB of HBM per device.

```python
import math
import jax
import jax.numpy as jnp
from jax import lax

E = 256
COL_DEV = 512
ROWS = 512
COLUMNS = 8192
N_COL = 16


def draw_counts(key, part):
    key = jax.random.fold_in(key, 11)
    first_key, second_key, third_key, fourth_key = jax.random.split(key, 4)
    levels = jax.random.randint(first_key, (ROWS, COLUMNS), 0, 13)
    raw_bits = jax.random.randint(second_key, (ROWS, COLUMNS), 0, 4096)
    values = jnp.right_shift(raw_bits, 12 - levels).astype(jnp.int32)
    top_row = jax.random.randint(third_key, (), 0, ROWS)
    top_column = jax.random.randint(fourth_key, (), 0, COLUMNS)
    return values.at[top_row, top_column].set(4095)


def with_ends(result, key, least, high):
    spot = [jax.random.randint(jax.random.fold_in(key, axis), (), 0, length) for axis, length in enumerate(result.shape)]
    longest = result.shape.index(max(result.shape))
    beside = spot[:longest] + [(spot[longest] + 1) % result.shape[longest]] + spot[longest + 1:]
    return result.at[tuple(spot)].set(least).at[tuple(beside)].set(high)


def level_of(rng, extent, pieces, smallest, largest):
    def one(axis_at, shards_of):
        heights = jax.random.uniform(jax.random.fold_in(jax.random.fold_in(rng, 6), axis_at), (shards_of,), jnp.float32, smallest / len(pieces), largest / len(pieces))
        return jnp.repeat(jnp.exp(heights), extent[axis_at] // shards_of).reshape((-1,) + (1,) * (len(extent) - axis_at - 1))

    factor_of = one(*pieces[0])
    for cut in pieces[1:]:
        factor_of = factor_of * one(*cut)
    return factor_of


def normal_values(own_key, shape, spread, limit, pieces=(), kind=jnp.bfloat16):
    array = jax.random.normal(own_key, shape, jnp.float32) * spread
    if len(pieces) > 0:
        array = level_of(own_key, shape, pieces, -0.22, 0.18) * array
    return jnp.clip(array, min=-limit, max=limit).astype(kind)


def setup_inputs(seed: int = 0, part: int = 0) -> dict:
    streams_of = jax.random.split(jax.random.key(seed), 8)
    part_splits = jax.random.split(jax.random.fold_in(streams_of[7], part), 8)
    counts = draw_counts(jax.random.fold_in(jax.random.fold_in(streams_of[7], part), 71), part)
    row_totals = with_ends(jax.random.randint(part_splits[1], (ROWS,), 1000, 1000000), jax.random.fold_in(part_splits[1], 1), 1000, 999999).astype(jnp.int32)
    column_totals = with_ends(jax.random.randint(part_splits[2], (COLUMNS,), 1000, 1000000), jax.random.fold_in(part_splits[2], 1), 1000, 999999).astype(jnp.int32)
    row_master = normal_values(part_splits[3], (ROWS, E), 0.25, 1.5, ((0, 16),), jnp.float32)
    row_history = jnp.clip(jnp.exp(math.log(0.1) - 2.3025851 * jax.random.uniform(part_splits[4], (ROWS, E), jnp.float32) ** level_of(part_splits[4], (ROWS, E), ((0, 16),), -0.2, 0.2)), 0.01, 0.1)
    column_master = normal_values(part_splits[5], (COLUMNS, E), 0.25, 1.5, ((0, 16),), jnp.float32)
    column_history = jnp.clip(jnp.exp(math.log(0.1) - 2.3025851 * jax.random.uniform(part_splits[6], (COLUMNS, E), jnp.float32) ** level_of(part_splits[6], (COLUMNS, E), ((0, 16),), -0.2, 0.2)), 0.01, 0.1)
    return {"counts": counts, "row_totals": row_totals, "column_totals": column_totals, "row_master": row_master, "row_history": row_history, "column_master": column_master, "column_history": column_history}


step_size = 2.0

def slope_terms(scores, counts, log_rows, log_columns, log_total):
    amounts = counts.astype(jnp.float32)
    log_count = jnp.log(jnp.maximum(amounts, 1.0))
    log_ratio = log_count + log_total - log_rows[:, None] - log_columns[None, :]
    confidence = 0.1 + 0.25 * jnp.sqrt(amounts)
    fitted = confidence * (scores - log_ratio)
    hinged = jax.nn.sigmoid(scores - log_ratio)
    return jnp.where(counts > 0, fitted, hinged).astype(jnp.bfloat16)

def adagrad(master, history, gradient):
    updated = history + gradient * gradient
    return (master - step_size * gradient / jnp.sqrt(updated), updated)

def reference(counts, row_totals, column_totals, row_master, row_history, column_master, column_history):
    row_floats = row_totals.astype(jnp.float32)
    log_total = jnp.log(jnp.sum(row_floats))
    log_rows = jnp.log(row_floats)
    row_copy = row_master.astype(jnp.bfloat16)

    def one_block(running, index):
        offset = (index * COL_DEV).astype(jnp.int32)
        block_counts = lax.dynamic_slice_in_dim(counts, offset, COL_DEV, 1)
        columns = lax.dynamic_slice_in_dim(column_master, offset, COL_DEV, 0).astype(jnp.bfloat16)
        log_columns = jnp.log(lax.dynamic_slice_in_dim(column_totals, offset, COL_DEV, 0).astype(jnp.float32))
        scores = jnp.dot(row_copy, columns.T, preferred_element_type=jnp.float32)
        slopes = slope_terms(scores, block_counts, log_rows, log_columns, log_total)
        running = running + jnp.dot(slopes, columns, preferred_element_type=jnp.float32)
        column_grad = jnp.dot(slopes.T, row_copy, preferred_element_type=jnp.float32) / ROWS
        return (running, column_grad)
    row_sum, column_grads = lax.scan(one_block, jnp.zeros((ROWS, E), jnp.float32), jnp.arange(N_COL, dtype=jnp.int32))
    column_grad = column_grads.reshape(COLUMNS, E)
    row_grad = row_sum / COLUMNS
    new_rows, new_row_hist = adagrad(row_master, row_history, row_grad)
    new_columns, new_column_hist = adagrad(column_master, column_history, column_grad)
    return (new_rows.astype(jnp.bfloat16), new_rows, new_row_hist, new_columns, new_column_hist)
```

```python
import functools

import jax
import jax.numpy as jnp
from jax import lax
from jax.experimental import pallas as pl
from jax.experimental.pallas import tpu as pltpu
from jax.sharding import PartitionSpec as P

step_size = 2.0
VMEM = pl.BlockSpec(memory_space=pltpu.VMEM)
ANY = pl.BlockSpec(memory_space=pl.ANY)
LIMIT = 56 * 1024 * 1024


def hop(value, bit, size):
    return lax.ppermute(value, "col", [(i, i ^ bit) for i in range(size)])


def slopes_kernel(chunk, counts, row_term, column_term, columns, *refs):
    pieces, (sent, kept, slopes, column_copy) = refs[:4], refs[4:]
    me = lax.axis_index("col")
    column_copy[...] = columns[...].astype(jnp.bfloat16)
    own_rows = counts.shape[3]
    group = chunk // own_rows
    steps = pieces[0].shape[0] // chunk
    for place in range(4):
        high, low = place // 2, place % 2
        at_x = lax.rem(lax.div(me, 2) + low, 2)
        at_core = lax.rem(me + high, 2)
        target = sent if high else kept

        def body(step, _, place=place, low=low, at_x=at_x, at_core=at_core, target=target):
            first = pl.multiple_of(step * chunk, chunk)
            rows = pieces[place][pl.ds(first, chunk), :]
            scores = lax.dot_general(
                rows, column_copy[...], (((1,), (1,)), ((), ())), preferred_element_type=jnp.float32
            )
            block = counts[pl.ds(step * group, group), at_x, at_core]
            amounts = block.reshape(chunk, block.shape[-1]).astype(jnp.float32)
            terms = row_term[pl.ds(place * steps * group + step * group, group)].reshape(chunk, 1)
            ratio = jnp.log(jnp.maximum(amounts, 1.0)) + terms - column_term[...]
            gap = scores - ratio
            fitted = (0.1 + 0.25 * jnp.sqrt(amounts)) * gap
            slope = jnp.where(amounts > 0, fitted, jax.nn.sigmoid(gap)).astype(jnp.bfloat16)
            slopes[place, pl.ds(first, chunk), :] = slope
            target[pl.ds(low * steps * chunk + first, chunk), :] = jnp.dot(
                slope, column_copy[...], preferred_element_type=jnp.float32
            ).astype(target.dtype)
            return 0

        if steps == 1:
            body(0, 0)
        else:
            lax.fori_loop(0, steps, body, 0)


def columns_kernel(total_rows, chunk, slopes, master, history, *refs):
    pieces, (new_master, new_history, total) = refs[:4], refs[4:]
    steps = pieces[0].shape[0] // chunk
    for place in range(4):

        def body(step, _, place=place):
            first = pl.multiple_of(step * chunk, chunk)
            part = lax.dot_general(
                slopes[place, pl.ds(first, chunk), :],
                pieces[place][pl.ds(first, chunk), :],
                (((0,), (0,)), ((), ())),
                preferred_element_type=jnp.float32,
            )
            total[...] = part if place == 0 and steps == 1 else total[...] + part
            return 0

        if steps == 1:
            body(0, 0)
        else:
            if place == 0:
                total[...] = jnp.zeros_like(total)
            lax.fori_loop(0, steps, body, 0)
    gradient = total[...] / total_rows
    updated = history[...] + gradient * gradient
    new_history[...] = updated
    new_master[...] = master[...] - step_size * gradient * lax.rsqrt(updated)


def place_kernel(*refs):
    pieces, out, sems = refs[:4], refs[4], refs[5]
    me = lax.axis_index("col")
    copies = []
    for place in range(4):
        at_x = lax.rem(lax.div(me, 2) + place % 2, 2)
        at_core = lax.rem(me + place // 2, 2)
        copies.append(pltpu.make_async_copy(pieces[place], out.at[:, at_x, at_core], sems.at[place]))
    for copy in copies:
        copy.start()
    for copy in copies:
        copy.wait()


def gather_group(value, size):
    me = lax.axis_index("col")
    held = [value]
    bit = size // 2
    while bit >= 4:
        held = held + [hop(v, bit, size) for v in held]
        bit //= 2
    group = size // 4
    bits = group.bit_length() - 1
    flip = [int(format(k, "b").zfill(bits)[::-1], 2) if bits else 0 for k in range(group)]
    by_offset = [held[flip[k]] for k in range(group)]
    place = lax.div(me, 4)
    for b in range(bits):
        turned = lax.rem(lax.div(place, 1 << b), 2) == 1
        by_offset = [jnp.where(turned, by_offset[k ^ (1 << b)], by_offset[k]) for k in range(group)]
    return jnp.stack(by_offset)


def per_device(
    counts, row_totals, column_totals, row_master, row_history, column_master, column_history
):
    size = lax.axis_size("col")
    me = lax.axis_index("col")
    total_rows, block_columns = counts.shape
    all_columns = block_columns * size
    own, width = row_master.shape
    group = size // 4
    group_rows = group * own
    chunk = 128

    row_floats = row_totals.astype(jnp.float32)
    row_term = (jnp.log(jnp.sum(row_floats)) - jnp.log(row_floats)).reshape(group, 2, 2, own)
    x_bit, core_bit = lax.rem(lax.div(me, 2), 2), lax.rem(me, 2)
    row_term = jnp.where(x_bit == 1, row_term[:, ::-1], row_term)
    row_term = jnp.where(core_bit == 1, row_term[:, :, ::-1], row_term)
    row_term = row_term.transpose(2, 1, 0, 3).reshape(4 * group, own, 1)
    column_term = jnp.log(column_totals.astype(jnp.float32)).reshape(1, block_columns)

    master = gather_group(row_master, size)
    history = gather_group(row_history, size)
    mine = master.reshape(group_rows, width).astype(jnp.bfloat16)
    beside = hop(mine, 2, size)
    pieces = (mine, beside, hop(mine, 1, size), hop(beside, 1, size))

    half = jax.ShapeDtypeStruct((2 * group_rows, width), jnp.bfloat16)
    kept_half = jax.ShapeDtypeStruct((2 * group_rows, width), jnp.float32)
    sent, kept, slopes = pl.pallas_call(
        functools.partial(slopes_kernel, chunk),
        out_shape=(half, kept_half, jax.ShapeDtypeStruct((4, group_rows, block_columns), jnp.bfloat16)),
        in_specs=[VMEM] * 8,
        out_specs=[VMEM] * 3,
        scratch_shapes=[pltpu.VMEM(column_master.shape, jnp.bfloat16)],
        compiler_params=pltpu.CompilerParams(vmem_limit_bytes=LIMIT),
        name="slopes",
    )(counts.reshape(group, 2, 2, own, block_columns), row_term, column_term, column_master, *pieces)

    part = kept + hop(sent, 1, size).astype(jnp.float32)
    part = part[:group_rows] + hop(part[group_rows:].astype(jnp.bfloat16), 2, size).astype(jnp.float32)
    bit = 4
    while bit < size:
        rounded = part.astype(jnp.bfloat16)
        part = rounded.astype(jnp.float32) + hop(rounded, bit, size).astype(jnp.float32)
        bit *= 2

    struct = jax.ShapeDtypeStruct(column_master.shape, jnp.float32)
    new_columns, new_column_history = pl.pallas_call(
        functools.partial(columns_kernel, total_rows, chunk),
        out_shape=(struct, struct),
        in_specs=[VMEM] * 7,
        out_specs=[VMEM] * 2,
        scratch_shapes=[pltpu.VMEM(column_master.shape, jnp.float32)],
        compiler_params=pltpu.CompilerParams(vmem_limit_bytes=LIMIT),
        cost_estimate=pl.CostEstimate(flops=4 * total_rows * block_columns * width, bytes_accessed=8 * 512 * 1024, transcendentals=0),
        name="columns",
    )(slopes, column_master, column_history, *pieces)

    gradient = part.reshape(group, own, width) / all_columns
    updated = history + gradient * gradient
    new_group = master - step_size * gradient / jnp.sqrt(updated)
    place = lax.div(me, 4)
    new_rows = lax.dynamic_index_in_dim(new_group, place, 0, keepdims=False)
    new_row_history = lax.dynamic_index_in_dim(updated, place, 0, keepdims=False)
    copy = new_group.astype(jnp.bfloat16)
    beside = hop(copy, 2, size)
    grid_rows = pl.pallas_call(
        place_kernel,
        out_shape=jax.ShapeDtypeStruct((group, 2, 2, own, width), jnp.bfloat16),
        in_specs=[ANY] * 4,
        out_specs=ANY,
        scratch_shapes=[pltpu.SemaphoreType.DMA((4,))],
        name="place",
    )(copy, beside, hop(copy, 1, size), hop(beside, 1, size))
    return (grid_rows.reshape(total_rows, width), new_rows, new_row_history, new_columns, new_column_history)


def solution(mesh):
    return jax.shard_map(
        per_device,
        mesh=mesh,
        in_specs=(
            P("parts", "col"),
            P("parts"),
            P(("parts", "col")),
            P(("parts", "col"), None),
            P(("parts", "col"), None),
            P(("parts", "col"), None),
            P(("parts", "col"), None),
        ),
        out_specs=(
            P("parts", None),
            P(("parts", "col"), None),
            P(("parts", "col"), None),
            P(("parts", "col"), None),
            P(("parts", "col"), None),
        ),
        check_vma=False,
    )
```

```python
import functools

import jax
import jax.numpy as jnp
from jax import lax
from jax.experimental import pallas as pl
from jax.experimental.pallas import tpu as pltpu
from jax.sharding import PartitionSpec as P

step_size = 2.0
VMEM = pl.BlockSpec(memory_space=pltpu.VMEM)
ANY = pl.BlockSpec(memory_space=pl.ANY)
PARAMS = pltpu.CompilerParams(vmem_limit_bytes=12 * 1024 * 1024)


def hop(value, bit, size):
    return lax.ppermute(value, "col", [(i, i ^ bit) for i in range(size)])


def near(value):
    return pltpu.with_memory_space_constraint(value, pltpu.VMEM)


def place_at(me, place):
    return lax.rem(lax.div(me, 2) + place % 2, 2), lax.rem(me + place // 2, 2)


def steps_of(count, body):
    if count == 1:
        body(0)
    else:
        pl.loop(0, count)(body)


def prepare_kernel(chunk, counts, row_totals, column_totals, columns, ratio, weight, column_copy):
    me = lax.axis_index("col")
    groups, own, owners = counts.shape[0], counts.shape[3], row_totals.shape[1]
    column_copy[...] = columns[...].astype(jnp.bfloat16)
    row_floats = row_totals[...].astype(jnp.float32)
    total = jnp.sum(jnp.sum(row_floats, axis=1, keepdims=True), axis=0, keepdims=True)
    row_terms = jnp.log(total) - jnp.log(row_floats)
    column_term = jnp.log(column_totals[...].astype(jnp.float32))
    owner = lax.broadcasted_iota(jnp.int32, row_terms.shape, 1)
    for place in range(4):
        at_x, at_core = place_at(me, place)

        def body(z, place=place, at_x=at_x, at_core=at_core):
            amounts = counts[z, at_x, at_core].astype(jnp.float32)
            here = owner == z * 4 + at_x * 2 + at_core
            row_term = jnp.sum(jnp.where(here, row_terms, 0.0), axis=1, keepdims=True)
            ratio[place, z] = jnp.log(jnp.maximum(amounts, 1.0)) + row_term - column_term
            weight[place, z] = jnp.where(amounts > 0, 0.1 + 0.25 * jnp.sqrt(amounts), 0.0)

        if groups <= 4:
            for z in range(groups):
                body(z)
        else:
            pl.loop(0, groups)(body)


def slopes_kernel(chunk, places, ratio, weight, column_copy, kept_rows, sent_rows, *refs):
    kept, sent, slopes = refs[-3:]
    group = chunk // ratio.shape[2]
    count = kept_rows.shape[0] // chunk
    for k, (place, source, target) in enumerate(zip(places, (kept_rows, sent_rows), (kept, sent))):

        def body(step, k=k, place=place, source=source, target=target):
            first = pl.multiple_of(step * chunk, chunk)
            scores = lax.dot_general(
                source[pl.ds(first, chunk), :],
                column_copy[...],
                (((1,), (1,)), ((), ())),
                preferred_element_type=jnp.float32,
            )
            at = pl.ds(step * group, group)
            gap = scores - ratio[place, at].reshape(scores.shape)
            confidence = weight[place, at].reshape(scores.shape)
            slope = jnp.where(confidence > 0, confidence * gap, jax.nn.sigmoid(gap)).astype(jnp.bfloat16)
            slopes[k, pl.ds(first, chunk), :] = slope
            target[pl.ds(first, chunk), :] = jnp.dot(
                slope, column_copy[...], preferred_element_type=jnp.float32
            ).astype(target.dtype)

        steps_of(count, body)


def columns_kernel(total_rows, chunk, early, late, master, history, *refs):
    pieces, (new_master, new_history, total) = refs[:4], refs[4:]
    count = pieces[0].shape[0] // chunk
    for place in range(4):
        slopes, k = (early, late)[place % 2], place // 2

        def body(step, place=place, slopes=slopes, k=k):
            first = pl.multiple_of(step * chunk, chunk)
            part = lax.dot_general(
                slopes[k, pl.ds(first, chunk), :],
                pieces[place][pl.ds(first, chunk), :],
                (((0,), (0,)), ((), ())),
                preferred_element_type=jnp.float32,
            )
            total[...] = part if place == 0 and count == 1 else total[...] + part

        if place == 0 and count > 1:
            total[...] = jnp.zeros_like(total)
        steps_of(count, body)
    gradient = total[...] / total_rows
    updated = history[...] + gradient * gradient
    new_history[...] = updated
    new_master[...] = master[...] - step_size * gradient * lax.rsqrt(updated)


def place_kernel(*refs):
    pieces, out = refs[:4], refs[4]
    me = lax.axis_index("col")
    for place in range(4):
        at_x, at_core = place_at(me, place)
        for z in range(out.shape[0]):
            out[z, at_x, at_core] = pieces[place][z]


def gather_group(value, size):
    place = lax.div(lax.axis_index("col"), 4)
    held = value[None]
    bit = size // 2
    while bit >= 4:
        other = hop(held, bit, size)
        upper = lax.rem(lax.div(place, bit // 4), 2) == 1
        low, high = jnp.where(upper, other, held), jnp.where(upper, held, other)
        held = jnp.stack([low, high], axis=1).reshape((2 * held.shape[0],) + held.shape[1:])
        bit //= 2
    return held


def per_device(
    counts, row_totals, column_totals, row_master, row_history, column_master, column_history
):
    size = lax.axis_size("col")
    me = lax.axis_index("col")
    total_rows, block_columns = counts.shape
    all_columns = block_columns * size
    own, width = row_master.shape
    group = size // 4
    group_rows = group * own
    chunk = 128
    ratio_type = pltpu.VMEM((4, group, own, block_columns), jnp.float32)

    master = gather_group(row_master, size)
    history = gather_group(row_history, size)
    mine = master.reshape(group_rows, width).astype(jnp.bfloat16)
    beside = hop(mine, 2, size)
    opposite = hop(mine, 1, size)
    corner = hop(beside, 1, size)

    ratio, weight, column_copy = pl.pallas_call(
        functools.partial(prepare_kernel, chunk),
        out_shape=(ratio_type, ratio_type, pltpu.VMEM(column_master.shape, jnp.bfloat16)),
        in_specs=[VMEM] * 4,
        out_specs=[VMEM] * 3,
        compiler_params=PARAMS,
        cost_estimate=pl.CostEstimate(flops=8 * counts.size, bytes_accessed=4 * counts.size, transcendentals=2 * counts.size),
        name="prepare",
    )(
        near(counts.reshape(group, 2, 2, own, block_columns)),
        near(row_totals.reshape(size, own).T),
        near(column_totals.reshape(1, block_columns)),
        near(column_master),
    )

    def slopes_of(places, kept_rows, sent_rows, *wait_for):
        return pl.pallas_call(
            functools.partial(slopes_kernel, chunk, places),
            out_shape=(
                pltpu.VMEM((group_rows, width), jnp.float32),
                pltpu.VMEM((group_rows, width), jnp.bfloat16),
                pltpu.VMEM((2, group_rows, block_columns), jnp.bfloat16),
            ),
            in_specs=[VMEM] * 5 + [ANY] * len(wait_for),
            out_specs=[VMEM] * 3,
            compiler_params=PARAMS,
            cost_estimate=pl.CostEstimate(flops=8 * group_rows * block_columns * width, bytes_accessed=0, transcendentals=4 * group_rows * block_columns),
            name="slopes",
        )(ratio, weight, column_copy, near(kept_rows), near(sent_rows), *wait_for)

    kept_early, sent_early, early = slopes_of((0, 2), mine, opposite)
    kept_late, sent_late, late = slopes_of((1, 3), beside, corner, history)

    part = kept_late + hop(sent_late, 1, size).astype(jnp.float32)
    other = hop(part.astype(jnp.bfloat16), 2, size)
    part = kept_early + hop(sent_early, 1, size).astype(jnp.float32) + other.astype(jnp.float32)
    bit = 4
    while bit < size:
        rounded = part.astype(jnp.bfloat16)
        part = rounded.astype(jnp.float32) + hop(rounded, bit, size).astype(jnp.float32)
        bit *= 2

    struct = jax.ShapeDtypeStruct(column_master.shape, jnp.float32)
    new_columns, new_column_history = pl.pallas_call(
        functools.partial(columns_kernel, total_rows, chunk),
        out_shape=(struct, struct),
        in_specs=[VMEM] * 8,
        out_specs=[VMEM] * 2,
        scratch_shapes=[pltpu.VMEM(column_master.shape, jnp.float32)],
        compiler_params=PARAMS,
        cost_estimate=pl.CostEstimate(flops=2 * total_rows * block_columns * width, bytes_accessed=4 * column_master.size * 4, transcendentals=0),
        name="columns",
    )(near(early), near(late), near(column_master), near(column_history), near(mine), near(beside), near(opposite), near(corner))

    gradient = part.reshape(group, own, width) / all_columns
    updated = history + gradient * gradient
    new_group = master - step_size * gradient / jnp.sqrt(updated)
    place = lax.div(me, 4)
    new_rows = lax.dynamic_index_in_dim(new_group, place, 0, keepdims=False)
    new_row_history = lax.dynamic_index_in_dim(updated, place, 0, keepdims=False)
    copy = new_group.astype(jnp.bfloat16)
    beside = hop(copy, 2, size)
    grid_rows = pl.pallas_call(
        place_kernel,
        out_shape=jax.ShapeDtypeStruct((group, 2, 2, own, width), jnp.bfloat16),
        in_specs=[VMEM] * 4,
        out_specs=VMEM,
        compiler_params=PARAMS,
        name="place",
    )(near(copy), near(beside), near(hop(copy, 1, size)), near(hop(beside, 1, size)))
    return (grid_rows.reshape(total_rows, width), new_rows, new_row_history, new_columns, new_column_history)


def solution(mesh):
    return jax.shard_map(
        per_device,
        mesh=mesh,
        in_specs=(
            P("parts", "col"),
            P("parts"),
            P(("parts", "col")),
            P(("parts", "col"), None),
            P(("parts", "col"), None),
            P(("parts", "col"), None),
            P(("parts", "col"), None),
        ),
        out_specs=(
            P("parts", None),
            P(("parts", "col"), None),
            P(("parts", "col"), None),
            P(("parts", "col"), None),
            P(("parts", "col"), None),
        ),
        check_vma=False,
    )
```

```python
import functools

import jax
import jax.numpy as jnp
from jax import lax
from jax.experimental import pallas as pl
from jax.experimental.pallas import tpu as pltpu
from jax.sharding import PartitionSpec as P

step_size = 2.0
VMEM = pl.BlockSpec(memory_space=pltpu.VMEM)
HBM = pl.BlockSpec(memory_space=pltpu.HBM)
ANY = pl.BlockSpec(memory_space=pl.ANY)
PARAMS = pltpu.CompilerParams(vmem_limit_bytes=16 * 1024 * 1024)


def hop(value, bit, size):
    return lax.ppermute(value, "col", [(i, i ^ bit) for i in range(size)])


def near(value):
    return pltpu.with_memory_space_constraint(value, pltpu.VMEM)


def far(value):
    return pltpu.with_memory_space_constraint(value, pltpu.HBM)


def place_at(me, place):
    return lax.rem(lax.div(me, 2) + place % 2, 2), lax.rem(me + place // 2, 2)


def steps_of(count, body):
    if count == 1:
        body(0)
    else:
        pl.loop(0, count)(body)


def prepare_kernel(counts, row_totals, column_totals, columns, _, ratio, weight, column_copy, *scratch):
    near_counts, near_rows, near_columns, near_copy, row_terms, sems = scratch
    me = lax.axis_index("col")
    groups, own = counts.shape[0], counts.shape[3]
    copies = [
        pltpu.make_async_copy(row_totals, near_rows, sems.at[0]),
        pltpu.make_async_copy(column_totals, near_columns, sems.at[1]),
        pltpu.make_async_copy(counts, near_counts, sems.at[2]),
        pltpu.make_async_copy(columns, near_copy, sems.at[3]),
    ]
    for copy in copies:
        copy.start()
    copies[0].wait()
    row_floats = near_rows[...].astype(jnp.float32)
    terms = jnp.log(jnp.sum(row_floats, axis=1, keepdims=True)) - jnp.log(row_floats)
    row_terms[...] = jnp.broadcast_to(terms, (128, terms.shape[1])).T.reshape(row_terms.shape)
    copies[1].wait()
    column_term = jnp.log(near_columns[...].astype(jnp.float32))
    copies[2].wait()
    for place in range(4):
        at_x, at_core = place_at(me, place)

        def body(z, place=place, at_x=at_x, at_core=at_core):
            amounts = near_counts[z, at_x, at_core].astype(jnp.float32)
            term = row_terms[z, at_x, at_core]
            term = jnp.concatenate([term] * (amounts.shape[1] // 128), axis=1)
            ratio[place, z] = jnp.log(jnp.maximum(amounts, 1.0)) + (term - column_term)
            weight[place, z] = jnp.where(amounts > 0, 0.1 + 0.25 * jnp.sqrt(amounts), 0.0)

        if groups <= 4:
            for z in range(groups):
                body(z)
        else:
            pl.loop(0, groups)(body)
    copies[3].wait()
    column_copy[...] = near_copy[...].astype(jnp.bfloat16)


def slopes_kernel(chunk, places, ratio, weight, column_copy, kept_rows, sent_rows, *refs):
    kept, sent, slopes = refs[-3:]
    group = chunk // ratio.shape[2]
    count = kept_rows.shape[0] // chunk
    for k, (place, source, target) in enumerate(zip(places, (kept_rows, sent_rows), (kept, sent))):

        def body(step, k=k, place=place, source=source, target=target):
            first = pl.multiple_of(step * chunk, chunk)
            scores = lax.dot_general(
                source[pl.ds(first, chunk), :],
                column_copy[...],
                (((1,), (1,)), ((), ())),
                preferred_element_type=jnp.float32,
            )
            at = pl.ds(step * group, group)
            gap = scores - ratio[place, at].reshape(scores.shape)
            confidence = weight[place, at].reshape(scores.shape)
            slope = jnp.where(confidence > 0, confidence * gap, jax.nn.sigmoid(gap)).astype(jnp.bfloat16)
            slopes[k, pl.ds(first, chunk), :] = slope
            target[pl.ds(first, chunk), :] = jnp.dot(
                slope, column_copy[...], preferred_element_type=jnp.float32
            ).astype(target.dtype)

        steps_of(count, body)


def columns_kernel(total_rows, chunk, early, late, master, history, *refs):
    pieces, (new_master, new_history, total) = refs[:4], refs[4:]
    count = pieces[0].shape[0] // chunk
    for place in range(4):
        slopes, k = (early, late)[place % 2], place // 2

        def body(step, place=place, slopes=slopes, k=k):
            first = pl.multiple_of(step * chunk, chunk)
            part = lax.dot_general(
                slopes[k, pl.ds(first, chunk), :],
                pieces[place][pl.ds(first, chunk), :],
                (((0,), (0,)), ((), ())),
                preferred_element_type=jnp.float32,
            )
            total[...] = part if place == 0 and count == 1 else total[...] + part

        if place == 0 and count > 1:
            total[...] = jnp.zeros_like(total)
        steps_of(count, body)
    gradient = total[...] / total_rows
    updated = history[...] + gradient * gradient
    new_history[...] = updated
    new_master[...] = master[...] - step_size * gradient * lax.rsqrt(updated)


def place_kernel(*refs):
    pieces, out = refs[:4], refs[4]
    me = lax.axis_index("col")
    for place in range(4):
        at_x, at_core = place_at(me, place)
        for z in range(out.shape[0]):
            out[z, at_x, at_core] = pieces[place][z]


def joined(held, other, bit):
    upper = lax.rem(lax.div(lax.axis_index("col"), bit), 2) == 1
    low, high = jnp.where(upper, other, held), jnp.where(upper, held, other)
    return jnp.stack([low, high], axis=1).reshape((2 * held.shape[0],) + held.shape[1:])


def per_device(
    counts, row_totals, column_totals, row_master, row_history, column_master, column_history
):
    size = lax.axis_size("col")
    me = lax.axis_index("col")
    total_rows, block_columns = counts.shape
    all_columns = block_columns * size
    own, width = row_master.shape
    group = size // 4
    group_rows = group * own
    chunk = 128
    ratio_type = pltpu.VMEM((4, group, own, block_columns), jnp.float32)

    bits = [size >> k for k in range(1, size.bit_length() - 2)]
    master, first_hop = row_master[None], None
    for bit in bits:
        other = hop(master, bit, size)
        first_hop = other if first_hop is None else first_hop
        master = joined(master, other, bit).astype(jnp.bfloat16)
    grid = (group, 2, 2, own)
    ratio, weight, column_copy = pl.pallas_call(
        prepare_kernel,
        out_shape=(ratio_type, ratio_type, pltpu.VMEM(column_master.shape, jnp.bfloat16)),
        in_specs=[HBM] * 4 + [ANY],
        out_specs=[VMEM] * 3,
        scratch_shapes=[
            pltpu.VMEM(grid + (block_columns,), jnp.int32),
            pltpu.VMEM((1, total_rows), jnp.int32),
            pltpu.VMEM((1, block_columns), jnp.int32),
            pltpu.VMEM(column_master.shape, jnp.float32),
            pltpu.VMEM(grid + (128,), jnp.float32),
            pltpu.SemaphoreType.DMA((4,)),
        ],
        compiler_params=PARAMS,
        cost_estimate=pl.CostEstimate(flops=8 * counts.size, bytes_accessed=4 * counts.size, transcendentals=2 * counts.size),
        name="prepare",
    )(
        far(counts.reshape(grid + (block_columns,))),
        far(row_totals.reshape(1, total_rows)),
        far(column_totals.reshape(1, block_columns)),
        far(column_master),
        first_hop,
    )

    master, column_copy = lax.optimization_barrier((master, column_copy))
    mine = master.reshape(group_rows, width)
    beside = hop(mine, 2, size)
    opposite = hop(mine, 1, size)
    corner = hop(beside, 1, size)

    def slopes_of(places, kept_rows, sent_rows, *wait_for):
        return pl.pallas_call(
            functools.partial(slopes_kernel, chunk, places),
            out_shape=(
                pltpu.VMEM((group_rows, width), jnp.float32),
                pltpu.VMEM((group_rows, width), jnp.bfloat16),
                pltpu.VMEM((2, group_rows, block_columns), jnp.bfloat16),
            ),
            in_specs=[VMEM] * 5 + [ANY] * len(wait_for),
            out_specs=[VMEM] * 3,
            compiler_params=PARAMS,
            cost_estimate=pl.CostEstimate(flops=8 * group_rows * block_columns * width, bytes_accessed=0, transcendentals=4 * group_rows * block_columns),
            name="slopes",
        )(ratio, weight, column_copy, near(kept_rows), near(sent_rows), *wait_for)

    kept_early, sent_early, early = slopes_of((0, 2), mine, opposite)
    kept_late, sent_late, late = slopes_of((1, 3), beside, corner, early)

    part = kept_late + hop(sent_late, 1, size).astype(jnp.float32)
    other = hop(part.astype(jnp.bfloat16), 2, size)
    part = kept_early + hop(sent_early, 1, size).astype(jnp.float32) + other.astype(jnp.float32)
    history = row_history.astype(jnp.bfloat16)[None]
    for bit in bits:
        rounded = part.astype(jnp.bfloat16)
        other = hop(jnp.concatenate([rounded, history.reshape(-1, width)]), bit, size)
        part = rounded.astype(jnp.float32) + other[:group_rows].astype(jnp.float32)
        history = joined(history, other[group_rows:].reshape(history.shape), bit)

    struct = jax.ShapeDtypeStruct(column_master.shape, jnp.float32)
    new_columns, new_column_history = pl.pallas_call(
        functools.partial(columns_kernel, total_rows, chunk),
        out_shape=(struct, struct),
        in_specs=[VMEM] * 8,
        out_specs=[VMEM] * 2,
        scratch_shapes=[pltpu.VMEM(column_master.shape, jnp.float32)],
        compiler_params=PARAMS,
        cost_estimate=pl.CostEstimate(flops=2 * total_rows * block_columns * width, bytes_accessed=4 * column_master.size * 4, transcendentals=0),
        name="columns",
    )(near(early), near(late), near(column_master), near(column_history), near(mine), near(beside), near(opposite), near(corner))

    def adagrad(master, history, gradient):
        updated = history + gradient * gradient
        return master - step_size * gradient * lax.rsqrt(updated), updated

    gradient = part.reshape(group, own, width) / all_columns
    own_gradient = lax.dynamic_index_in_dim(gradient, lax.div(me, 4), 0, keepdims=False)
    new_rows, new_row_history = adagrad(row_master, row_history, own_gradient)
    copy = adagrad(master.astype(jnp.float32), history.astype(jnp.float32), gradient)[0].astype(jnp.bfloat16)
    beside = hop(copy, 2, size)
    grid_rows = pl.pallas_call(
        place_kernel,
        out_shape=jax.ShapeDtypeStruct((group, 2, 2, own, width), jnp.bfloat16),
        in_specs=[VMEM] * 4,
        out_specs=VMEM,
        compiler_params=PARAMS,
        name="place",
    )(near(copy), near(beside), near(hop(copy, 1, size)), near(hop(beside, 1, size)))
    return (grid_rows.reshape(total_rows, width), new_rows, new_row_history, new_columns, new_column_history)


def solution(mesh):
    return jax.shard_map(
        per_device,
        mesh=mesh,
        in_specs=(
            P("parts", "col"),
            P("parts"),
            P(("parts", "col")),
            P(("parts", "col"), None),
            P(("parts", "col"), None),
            P(("parts", "col"), None),
            P(("parts", "col"), None),
        ),
        out_specs=(
            P("parts", None),
            P(("parts", "col"), None),
            P(("parts", "col"), None),
            P(("parts", "col"), None),
            P(("parts", "col"), None),
        ),
        check_vma=False,
    )
```

```python
import functools

import jax
import jax.numpy as jnp
from jax import lax
from jax.experimental import pallas as pl
from jax.experimental.pallas import tpu as pltpu
from jax.sharding import PartitionSpec as P

step_size = 2.0
VMEM = pl.BlockSpec(memory_space=pltpu.VMEM)
HBM = pl.BlockSpec(memory_space=pltpu.HBM)
ANY = pl.BlockSpec(memory_space=pl.ANY)
PARAMS = pltpu.CompilerParams(vmem_limit_bytes=16 * 1024 * 1024)


def hop(value, bit, size):
    return lax.ppermute(value, "col", [(i, i ^ (bit | 1)) for i in range(size)])


def parity(value):
    for shift in (8, 4, 2, 1):
        value = value ^ (value >> shift)
    return value & 1


def near(value):
    return pltpu.with_memory_space_constraint(value, pltpu.VMEM)


def far(value):
    return pltpu.with_memory_space_constraint(value, pltpu.HBM)


def place_at(place, z):
    me = lax.axis_index("col")
    at_x = ((me >> 1) + place) & 1
    return at_x, (parity(me) + (place >> 1) + at_x + parity(z)) & 1


def steps_of(count, body):
    if count == 1:
        body(0)
    else:
        pl.loop(0, count)(body)


def prepare_kernel(counts, row_totals, column_totals, columns, _, ratio, weight, column_copy, *scratch):
    near_counts, near_rows, near_columns, near_copy, row_terms, sems = scratch
    groups, own = counts.shape[0], counts.shape[3]
    copies = [
        pltpu.make_async_copy(row_totals, near_rows, sems.at[0]),
        pltpu.make_async_copy(column_totals, near_columns, sems.at[1]),
        pltpu.make_async_copy(counts, near_counts, sems.at[2]),
        pltpu.make_async_copy(columns, near_copy, sems.at[3]),
    ]
    for copy in copies:
        copy.start()
    copies[0].wait()
    row_floats = near_rows[...].astype(jnp.float32)
    terms = jnp.log(jnp.sum(row_floats, axis=1, keepdims=True)) - jnp.log(row_floats)
    row_terms[...] = jnp.broadcast_to(terms, (128, terms.shape[1])).T.reshape(row_terms.shape)
    copies[1].wait()
    column_term = jnp.log(near_columns[...].astype(jnp.float32))
    copies[2].wait()
    for place in range(4):

        def body(z, place=place):
            at_x, at_core = place_at(place, z)
            amounts = near_counts[z, at_x, at_core].astype(jnp.float32)
            term = row_terms[z, at_x, at_core]
            term = jnp.concatenate([term] * (amounts.shape[1] // 128), axis=1)
            ratio[place, z] = jnp.log(jnp.maximum(amounts, 1.0)) + (term - column_term)
            weight[place, z] = jnp.where(amounts > 0, 0.1 + 0.25 * jnp.sqrt(amounts), 0.0)

        if groups <= 4:
            for z in range(groups):
                body(z)
        else:
            pl.loop(0, groups)(body)
    copies[3].wait()
    column_copy[...] = near_copy[...].astype(jnp.bfloat16)


def slopes_kernel(chunk, places, ratio, weight, column_copy, kept_rows, sent_rows, *refs):
    kept, sent, slopes = refs[-3:]
    group = chunk // ratio.shape[2]
    count = kept_rows.shape[0] // chunk
    for k, (place, source, target) in enumerate(zip(places, (kept_rows, sent_rows), (kept, sent))):

        def body(step, k=k, place=place, source=source, target=target):
            first = pl.multiple_of(step * chunk, chunk)
            scores = lax.dot_general(
                source[pl.ds(first, chunk), :],
                column_copy[...],
                (((1,), (1,)), ((), ())),
                preferred_element_type=jnp.float32,
            )
            at = pl.ds(step * group, group)
            gap = scores - ratio[place, at].reshape(scores.shape)
            confidence = weight[place, at].reshape(scores.shape)
            slope = jnp.where(confidence > 0, confidence * gap, jax.nn.sigmoid(gap)).astype(jnp.bfloat16)
            slopes[k, pl.ds(first, chunk), :] = slope
            target[pl.ds(first, chunk), :] = jnp.dot(
                slope, column_copy[...], preferred_element_type=jnp.float32
            ).astype(target.dtype)

        steps_of(count, body)


def columns_kernel(total_rows, chunk, early, late, master, history, *refs):
    pieces, (new_master, new_history, total) = refs[:4], refs[4:]
    count = pieces[0].shape[0] // chunk
    for place in range(4):
        slopes, k = (early, late)[place % 2], place // 2

        def body(step, place=place, slopes=slopes, k=k):
            first = pl.multiple_of(step * chunk, chunk)
            part = lax.dot_general(
                slopes[k, pl.ds(first, chunk), :],
                pieces[place][pl.ds(first, chunk), :],
                (((0,), (0,)), ((), ())),
                preferred_element_type=jnp.float32,
            )
            total[...] = part if place == 0 and count == 1 else total[...] + part

        if place == 0 and count > 1:
            total[...] = jnp.zeros_like(total)
        steps_of(count, body)
    gradient = total[...] / total_rows
    updated = history[...] + gradient * gradient
    new_history[...] = updated
    new_master[...] = master[...] - step_size * gradient * lax.rsqrt(updated)


def place_kernel(*refs):
    pieces, out = refs[:4], refs[4]
    for place in range(4):
        for z in range(out.shape[0]):
            at_x, at_core = place_at(place, z)
            out[z, at_x, at_core] = pieces[place][z]


def joined(held, other, bit):
    upper = lax.rem(lax.div(lax.axis_index("col"), bit), 2) == 1
    low, high = jnp.where(upper, other, held), jnp.where(upper, held, other)
    return jnp.stack([low, high], axis=1).reshape((2 * held.shape[0],) + held.shape[1:])


def per_device(
    counts, row_totals, column_totals, row_master, row_history, column_master, column_history
):
    size = lax.axis_size("col")
    me = lax.axis_index("col")
    total_rows, block_columns = counts.shape
    all_columns = block_columns * size
    own, width = row_master.shape
    group = size // 4
    group_rows = group * own
    chunk = 128
    ratio_type = pltpu.VMEM((4, group, own, block_columns), jnp.float32)

    bits = [size >> k for k in range(1, size.bit_length() - 2)]
    master, first_hop = row_master[None], None
    for bit in bits:
        other = hop(master, bit, size)
        first_hop = other if first_hop is None else first_hop
        master = joined(master, other, bit).astype(jnp.bfloat16)
    grid = (group, 2, 2, own)
    ratio, weight, column_copy = pl.pallas_call(
        prepare_kernel,
        out_shape=(ratio_type, ratio_type, pltpu.VMEM(column_master.shape, jnp.bfloat16)),
        in_specs=[HBM] * 4 + [ANY],
        out_specs=[VMEM] * 3,
        scratch_shapes=[
            pltpu.VMEM(grid + (block_columns,), jnp.int32),
            pltpu.VMEM((1, total_rows), jnp.int32),
            pltpu.VMEM((1, block_columns), jnp.int32),
            pltpu.VMEM(column_master.shape, jnp.float32),
            pltpu.VMEM(grid + (128,), jnp.float32),
            pltpu.SemaphoreType.DMA((4,)),
        ],
        compiler_params=PARAMS,
        cost_estimate=pl.CostEstimate(flops=8 * counts.size, bytes_accessed=4 * counts.size, transcendentals=2 * counts.size),
        name="prepare",
    )(
        far(counts.reshape(grid + (block_columns,))),
        far(row_totals.reshape(1, total_rows)),
        far(column_totals.reshape(1, block_columns)),
        far(column_master),
        first_hop,
    )

    master, column_copy = lax.optimization_barrier((master, column_copy))
    mine = master.reshape(group_rows, width)
    beside = hop(mine, 2, size)
    opposite = hop(mine, 1, size)
    corner = hop(beside, 1, size)

    def slopes_of(places, kept_rows, sent_rows, *wait_for):
        return pl.pallas_call(
            functools.partial(slopes_kernel, chunk, places),
            out_shape=(
                pltpu.VMEM((group_rows, width), jnp.float32),
                pltpu.VMEM((group_rows, width), jnp.bfloat16),
                pltpu.VMEM((2, group_rows, block_columns), jnp.bfloat16),
            ),
            in_specs=[VMEM] * 5 + [ANY] * len(wait_for),
            out_specs=[VMEM] * 3,
            compiler_params=PARAMS,
            cost_estimate=pl.CostEstimate(flops=8 * group_rows * block_columns * width, bytes_accessed=0, transcendentals=4 * group_rows * block_columns),
            name="slopes",
        )(ratio, weight, column_copy, near(kept_rows), near(sent_rows), *wait_for)

    kept_early, sent_early, early = slopes_of((0, 2), mine, opposite)
    kept_late, sent_late, late = slopes_of((1, 3), beside, corner, early)

    part = kept_late + hop(sent_late, 1, size).astype(jnp.float32)
    other = hop(part.astype(jnp.bfloat16), 2, size)
    part = kept_early + hop(sent_early, 1, size).astype(jnp.float32) + other.astype(jnp.float32)
    history = row_history.astype(jnp.bfloat16)[None]
    for bit in bits:
        rounded = part.astype(jnp.bfloat16)
        other = hop(jnp.concatenate([rounded, history.reshape(-1, width)]), bit, size)
        part = rounded.astype(jnp.float32) + other[:group_rows].astype(jnp.float32)
        history = joined(history, other[group_rows:].reshape(history.shape), bit)

    struct = jax.ShapeDtypeStruct(column_master.shape, jnp.float32)
    new_columns, new_column_history = pl.pallas_call(
        functools.partial(columns_kernel, total_rows, chunk),
        out_shape=(struct, struct),
        in_specs=[VMEM] * 8,
        out_specs=[VMEM] * 2,
        scratch_shapes=[pltpu.VMEM(column_master.shape, jnp.float32)],
        compiler_params=PARAMS,
        cost_estimate=pl.CostEstimate(flops=2 * total_rows * block_columns * width, bytes_accessed=4 * column_master.size * 4, transcendentals=0),
        name="columns",
    )(near(early), near(late), near(column_master), near(column_history), near(mine), near(beside), near(opposite), near(corner))

    def adagrad(master, history, gradient):
        updated = history + gradient * gradient
        return master - step_size * gradient * lax.rsqrt(updated), updated

    gradient = part.reshape(group, own, width) / all_columns
    own_gradient = lax.dynamic_index_in_dim(gradient, lax.div(me, 4), 0, keepdims=False)
    new_rows, new_row_history = adagrad(row_master, row_history, own_gradient)
    copy = adagrad(master.astype(jnp.float32), history.astype(jnp.float32), gradient)[0].astype(jnp.bfloat16)
    beside = hop(copy, 2, size)
    grid_rows = pl.pallas_call(
        place_kernel,
        out_shape=jax.ShapeDtypeStruct((group, 2, 2, own, width), jnp.bfloat16),
        in_specs=[VMEM] * 4,
        out_specs=VMEM,
        compiler_params=PARAMS,
        name="place",
    )(near(copy), near(beside), near(hop(copy, 1, size)), near(hop(beside, 1, size)))
    return (grid_rows.reshape(total_rows, width), new_rows, new_row_history, new_columns, new_column_history)


def solution(mesh):
    return jax.shard_map(
        per_device,
        mesh=mesh,
        in_specs=(
            P("parts", "col"),
            P("parts"),
            P(("parts", "col")),
            P(("parts", "col"), None),
            P(("parts", "col"), None),
            P(("parts", "col"), None),
            P(("parts", "col"), None),
        ),
        out_specs=(
            P("parts", None),
            P(("parts", "col"), None),
            P(("parts", "col"), None),
            P(("parts", "col"), None),
            P(("parts", "col"), None),
        ),
        check_vma=False,
    )
```

```python
import functools

import jax
import jax.numpy as jnp
from jax import lax
from jax.experimental import pallas as pl
from jax.experimental.pallas import tpu as pltpu
from jax.sharding import PartitionSpec as P

step_size = 2.0
VMEM = pl.BlockSpec(memory_space=pltpu.VMEM)
HBM = pl.BlockSpec(memory_space=pltpu.HBM)
ANY = pl.BlockSpec(memory_space=pl.ANY)
PARAMS = pltpu.CompilerParams(vmem_limit_bytes=16 * 1024 * 1024)


def parity(value):
    for shift in (8, 4, 2, 1):
        value = value ^ (value >> shift)
    return value & 1


def hop(value, bits, size):
    pairs = [(i, i ^ (bits[parity(i)] | 1)) for i in range(size)]
    return lax.ppermute(value, "col", pairs)


CORE, SPLIT, SUM = (1, 1), (2, 4), (4, 2)


def near(value):
    return pltpu.with_memory_space_constraint(value, pltpu.VMEM)


def far(value):
    return pltpu.with_memory_space_constraint(value, pltpu.HBM)


def place_at(place, g):
    me = lax.axis_index("col")
    odd = parity(me) ^ (place >> 1)
    one, two = (me >> 1) & 1, (me >> 2) & 1
    split, last, rest = (one + odd * (two - one)) ^ (place & 1), g & 1, g >> 1
    bit_one, bit_two = split + odd * (last - split), last + odd * (split - last)
    return rest, bit_two, bit_one, odd ^ bit_one ^ bit_two ^ parity(rest)


def steps_of(count, body):
    if count == 1:
        body(0)
    else:
        pl.loop(0, count)(body)


def prepare_kernel(counts, row_totals, column_totals, columns, _, ratio, weight, column_copy, *scratch):
    near_counts, near_rows, near_columns, near_copy, row_terms, sems = scratch
    groups = ratio.shape[1]
    copies = [
        pltpu.make_async_copy(row_totals, near_rows, sems.at[0]),
        pltpu.make_async_copy(column_totals, near_columns, sems.at[1]),
        pltpu.make_async_copy(counts, near_counts, sems.at[2]),
        pltpu.make_async_copy(columns, near_copy, sems.at[3]),
    ]
    for copy in copies:
        copy.start()
    copies[0].wait()
    row_floats = near_rows[...].astype(jnp.float32)
    terms = jnp.log(jnp.sum(row_floats, axis=1, keepdims=True)) - jnp.log(row_floats)
    row_terms[...] = jnp.broadcast_to(terms, (128, terms.shape[1])).T.reshape(row_terms.shape)
    copies[1].wait()
    column_term = jnp.log(near_columns[...].astype(jnp.float32))
    copies[2].wait()
    for place in range(4):

        def body(g, place=place):
            at = place_at(place, g)
            amounts = near_counts[at].astype(jnp.float32)
            term = row_terms[at]
            term = jnp.concatenate([term] * (amounts.shape[1] // 128), axis=1)
            ratio[place, g] = jnp.log(jnp.maximum(amounts, 1.0)) + (term - column_term)
            weight[place, g] = jnp.where(amounts > 0, 0.1 + 0.25 * jnp.sqrt(amounts), 0.0)

        if groups <= 4:
            for g in range(groups):
                body(g)
        else:
            pl.loop(0, groups)(body)
    copies[3].wait()
    column_copy[...] = near_copy[...].astype(jnp.bfloat16)


def slopes_kernel(chunk, places, ratio, weight, column_copy, *refs):
    rows, outs = refs[: len(places)], refs[len(places) :]
    group = chunk // ratio.shape[2]
    count = rows[0].shape[0] // chunk
    for k, place in enumerate(places):

        def body(step, place=place, source=rows[k], target=outs[2 * k], slopes=outs[2 * k + 1]):
            first = pl.multiple_of(step * chunk, chunk)
            scores = lax.dot_general(
                source[pl.ds(first, chunk), :],
                column_copy[...],
                (((1,), (1,)), ((), ())),
                preferred_element_type=jnp.float32,
            )
            at = pl.ds(step * group, group)
            gap = scores - ratio[place, at].reshape(scores.shape)
            confidence = weight[place, at].reshape(scores.shape)
            slope = jnp.where(confidence > 0, confidence * gap, jax.nn.sigmoid(gap)).astype(jnp.bfloat16)
            slopes[pl.ds(first, chunk), :] = slope
            target[pl.ds(first, chunk), :] = jnp.dot(
                slope, column_copy[...], preferred_element_type=jnp.float32
            ).astype(target.dtype)

        steps_of(count, body)


def columns_kernel(total_rows, chunk, master, history, *refs):
    pieces, slopes, (new_master, new_history, total) = refs[:4], refs[4:8], refs[8:]
    count = pieces[0].shape[0] // chunk
    for place in range(4):

        def body(step, place=place):
            first = pl.multiple_of(step * chunk, chunk)
            part = lax.dot_general(
                slopes[place][pl.ds(first, chunk), :],
                pieces[place][pl.ds(first, chunk), :],
                (((0,), (0,)), ((), ())),
                preferred_element_type=jnp.float32,
            )
            total[...] = part if place == 0 and count == 1 else total[...] + part

        if place == 0 and count > 1:
            total[...] = jnp.zeros_like(total)
        steps_of(count, body)
    gradient = total[...] / total_rows
    updated = history[...] + gradient * gradient
    new_history[...] = updated
    new_master[...] = master[...] - step_size * gradient * lax.rsqrt(updated)


def place_kernel(*refs):
    pieces, out = refs[:4], refs[4]
    for place in range(4):
        for g in range(pieces[0].shape[0]):
            out[place_at(place, g)] = pieces[place][g]


def joined(held, other, upper):
    low, high = jnp.where(upper, other, held), jnp.where(upper, held, other)
    return jnp.stack([low, high], axis=1).reshape((2 * held.shape[0],) + held.shape[1:])


def per_device(
    counts, row_totals, column_totals, row_master, row_history, column_master, column_history
):
    size = lax.axis_size("col")
    me = lax.axis_index("col")
    total_rows, block_columns = counts.shape
    all_columns = block_columns * size
    own, width = row_master.shape
    group = size // 4
    group_rows = group * own
    chunk = 128
    ratio_type = pltpu.VMEM((4, group, own, block_columns), jnp.float32)

    odd = parity(me)
    last = jnp.where(odd == 1, me >> 1, me >> 2) & 1
    place = (me >> 3) * 2 + last
    top = [size >> k for k in range(1, size.bit_length() - 3)]
    steps = [((bit, bit), (me & bit) != 0) for bit in top] + [(SUM, last != 0)]
    master, first_hop = row_master[None], None
    for bits, upper in steps:
        other = hop(master, bits, size)
        first_hop = other if first_hop is None else first_hop
        master = joined(master, other, upper).astype(jnp.bfloat16)
    grid = (group // 2, 2, 2, 2, own)
    ratio, weight, column_copy = pl.pallas_call(
        prepare_kernel,
        out_shape=(ratio_type, ratio_type, pltpu.VMEM(column_master.shape, jnp.bfloat16)),
        in_specs=[HBM] * 4 + [ANY],
        out_specs=[VMEM] * 3,
        scratch_shapes=[
            pltpu.VMEM(grid + (block_columns,), jnp.int32),
            pltpu.VMEM((1, total_rows), jnp.int32),
            pltpu.VMEM((1, block_columns), jnp.int32),
            pltpu.VMEM(column_master.shape, jnp.float32),
            pltpu.VMEM(grid + (128,), jnp.float32),
            pltpu.SemaphoreType.DMA((4,)),
        ],
        compiler_params=PARAMS,
        cost_estimate=pl.CostEstimate(flops=8 * counts.size, bytes_accessed=4 * counts.size, transcendentals=2 * counts.size),
        name="prepare",
    )(
        far(counts.reshape(grid + (block_columns,))),
        far(row_totals.reshape(1, total_rows)),
        far(column_totals.reshape(1, block_columns)),
        far(column_master),
        first_hop,
    )

    master, column_copy = lax.optimization_barrier((master, column_copy))
    mine = master.reshape(group_rows, width)
    beside = hop(mine, SPLIT, size)
    opposite = hop(mine, CORE, size)

    def slopes_of(places, *rows):
        types = [(pltpu.VMEM((group_rows, width), jnp.float32 if place < 2 else jnp.bfloat16), pltpu.VMEM((group_rows, block_columns), jnp.bfloat16)) for place in places]
        return pl.pallas_call(
            functools.partial(slopes_kernel, chunk, places),
            out_shape=sum(types, ()),
            in_specs=[VMEM] * (3 + len(places)),
            out_specs=[VMEM] * (2 * len(places)),
            compiler_params=PARAMS,
            cost_estimate=pl.CostEstimate(flops=4 * len(places) * group_rows * block_columns * width, bytes_accessed=0, transcendentals=2 * len(places) * group_rows * block_columns),
            name="slopes",
        )(ratio, weight, column_copy, *[near(r) for r in rows])

    kept_early, slopes_0, sent_early, slopes_2 = slopes_of((0, 2), mine, opposite)
    beside, kept_early = lax.optimization_barrier((beside, kept_early))
    corner = hop(beside, CORE, size)
    kept_late, slopes_1 = slopes_of((1,), beside)
    sent_late, slopes_3 = slopes_of((3,), corner)

    part = kept_late + hop(sent_late, CORE, size).astype(jnp.float32)
    other = hop(part.astype(jnp.bfloat16), SPLIT, size)
    part = kept_early + hop(sent_early, CORE, size).astype(jnp.float32) + other.astype(jnp.float32)
    history = row_history.astype(jnp.bfloat16)[None]
    for bits, upper in steps:
        rounded = part.astype(jnp.bfloat16)
        other = hop(jnp.concatenate([rounded, history.reshape(-1, width)]), bits, size)
        part = rounded.astype(jnp.float32) + other[:group_rows].astype(jnp.float32)
        history = joined(history, other[group_rows:].reshape(history.shape), upper)

    struct = jax.ShapeDtypeStruct(column_master.shape, jnp.float32)
    new_columns, new_column_history = pl.pallas_call(
        functools.partial(columns_kernel, total_rows, chunk),
        out_shape=(struct, struct),
        in_specs=[VMEM] * 10,
        out_specs=[VMEM] * 2,
        scratch_shapes=[pltpu.VMEM(column_master.shape, jnp.float32)],
        compiler_params=PARAMS,
        cost_estimate=pl.CostEstimate(flops=2 * total_rows * block_columns * width, bytes_accessed=4 * column_master.size * 4, transcendentals=0),
        name="columns",
    )(*[near(v) for v in (column_master, column_history, mine, beside, opposite, corner, slopes_0, slopes_1, slopes_2, slopes_3)])

    def adagrad(master, history, gradient):
        updated = history + gradient * gradient
        return master - step_size * gradient * lax.rsqrt(updated), updated

    gradient = part.reshape(group, own, width) / all_columns
    own_gradient = lax.dynamic_index_in_dim(gradient, place, 0, keepdims=False)
    new_rows, new_row_history = adagrad(row_master, row_history, own_gradient)
    copy = adagrad(master.astype(jnp.float32), history.astype(jnp.float32), gradient)[0].astype(jnp.bfloat16)
    beside = hop(copy, SPLIT, size)
    grid_rows = pl.pallas_call(
        place_kernel,
        out_shape=jax.ShapeDtypeStruct(grid + (width,), jnp.bfloat16),
        in_specs=[VMEM] * 4,
        out_specs=VMEM,
        compiler_params=PARAMS,
        name="place",
    )(near(copy), near(beside), near(hop(copy, CORE, size)), near(hop(beside, CORE, size)))
    return (grid_rows.reshape(total_rows, width), new_rows, new_row_history, new_columns, new_column_history)


def solution(mesh):
    return jax.shard_map(
        per_device,
        mesh=mesh,
        in_specs=(
            P("parts", "col"),
            P("parts"),
            P(("parts", "col")),
            P(("parts", "col"), None),
            P(("parts", "col"), None),
            P(("parts", "col"), None),
            P(("parts", "col"), None),
        ),
        out_specs=(
            P("parts", None),
            P(("parts", "col"), None),
            P(("parts", "col"), None),
            P(("parts", "col"), None),
            P(("parts", "col"), None),
        ),
        check_vma=False,
    )
```

```python
import functools

import jax
import jax.numpy as jnp
from jax import lax
from jax.experimental import pallas as pl
from jax.experimental.pallas import tpu as pltpu
from jax.sharding import PartitionSpec as P

step_size = 2.0
VMEM = pl.BlockSpec(memory_space=pltpu.VMEM)
HBM = pl.BlockSpec(memory_space=pltpu.HBM)
ANY = pl.BlockSpec(memory_space=pl.ANY)
PARAMS = pltpu.CompilerParams(vmem_limit_bytes=20 * 1024 * 1024)


def parity(value):
    for shift in (8, 4, 2, 1):
        value = value ^ (value >> shift)
    return value & 1


def hop(value, bits, size):
    pairs = [(i, i ^ (bits[parity(i)] | 1)) for i in range(size)]
    return lax.ppermute(value, "col", pairs)


CORE, SPLIT, SUM = (1, 1), (2, 4), (4, 2)


def near(value):
    return pltpu.with_memory_space_constraint(value, pltpu.VMEM)


def far(value):
    return pltpu.with_memory_space_constraint(value, pltpu.HBM)


def place_at(place, g):
    me = lax.axis_index("col")
    odd = parity(me) ^ (place >> 1)
    one, two = (me >> 1) & 1, (me >> 2) & 1
    split, last, rest = (one + odd * (two - one)) ^ (place & 1), g & 1, g >> 1
    bit_one, bit_two = split + odd * (last - split), last + odd * (split - last)
    return rest, bit_two, bit_one, odd ^ bit_one ^ bit_two ^ parity(rest)


def steps_of(count, body):
    if count == 1:
        body(0)
    else:
        pl.loop(0, count)(body)


def prepare_kernel(counts, row_totals, column_totals, columns, _, kept_0, kept_1, sent_0, sent_1, column_copy, *scratch):
    near_counts, near_rows, near_columns, near_copy, row_terms, sems = scratch
    groups = kept_0.shape[1]
    copies = [
        pltpu.make_async_copy(row_totals, near_rows, sems.at[0]),
        pltpu.make_async_copy(column_totals, near_columns, sems.at[1]),
        pltpu.make_async_copy(counts, near_counts, sems.at[2]),
        pltpu.make_async_copy(columns, near_copy, sems.at[3]),
    ]
    for copy in copies:
        copy.start()
    copies[0].wait()
    row_floats = near_rows[...].astype(jnp.float32)
    terms = jnp.log(jnp.sum(row_floats, axis=1, keepdims=True)) - jnp.log(row_floats)
    row_terms[...] = jnp.broadcast_to(terms, (128, terms.shape[1])).T.reshape(row_terms.shape)
    copies[1].wait()
    column_term = jnp.log(near_columns[...].astype(jnp.float32))
    copies[2].wait()
    for place in range(4):

        def body(g, place=place):
            at = place_at(place, g)
            amounts = near_counts[at].astype(jnp.float32)
            term = row_terms[at]
            term = jnp.concatenate([term] * (amounts.shape[1] // 128), axis=1)
            target = (kept_0, kept_1, sent_0, sent_1)[place]
            target[0, g] = jnp.log(jnp.maximum(amounts, 1.0)) + (term - column_term)
            target[1, g] = jnp.where(amounts > 0, 0.1 + 0.25 * jnp.sqrt(amounts), 0.0)

        if groups <= 4:
            for g in range(groups):
                body(g)
        else:
            pl.loop(0, groups)(body)
    copies[3].wait()
    column_copy[...] = near_copy[...].astype(jnp.bfloat16)


def slopes_of(rows, columns, terms, step, chunk):
    group = chunk // terms.shape[2]
    at = pl.ds(step * group, group)
    scores = lax.dot_general(rows, columns, (((1,), (1,)), ((), ())), preferred_element_type=jnp.float32)
    gap = scores - terms[0, at].reshape(scores.shape)
    confidence = terms[1, at].reshape(scores.shape)
    return jnp.where(confidence > 0, confidence * gap, jax.nn.sigmoid(gap)).astype(jnp.bfloat16)


def rows_kernel(chunk, rows, kept, received, columns, other_columns, gradient, slopes):
    def body(step):
        at = pl.ds(pl.multiple_of(step * chunk, chunk), chunk)
        own = slopes_of(rows[at, :], columns[...], kept, step, chunk)
        slopes[at, :] = own
        gradient[at, :] = jnp.dot(own, columns[...], preferred_element_type=jnp.float32)
        other = slopes_of(rows[at, :], other_columns[...], received, step, chunk)
        gradient[at, :] += jnp.dot(other, other_columns[...], preferred_element_type=jnp.float32)

    steps_of(rows.shape[0] // chunk, body)


def columns_kernel(total_rows, chunk, master, history, columns, sent_0, sent_1, mine, beside, others, slopes_0, slopes_1, *outs):
    new_master, new_history, total = outs
    group_rows = mine.shape[0]
    total[...] = jnp.zeros_like(total)

    def body(step):
        first = pl.multiple_of(step * chunk, chunk)
        at = pl.ds(first, chunk)
        part = total[...]
        for place in range(2):
            rows = (mine, beside)[place][at, :]
            own = (slopes_0, slopes_1)[place][at, :]
            part += lax.dot_general(own, rows, (((0,), (0,)), ((), ())), preferred_element_type=jnp.float32)
            rows = others[pl.ds(place * group_rows + first, chunk), :]
            own = slopes_of(rows, columns[...], (sent_0, sent_1)[place], step, chunk)
            part += lax.dot_general(own, rows, (((0,), (0,)), ((), ())), preferred_element_type=jnp.float32)
        total[...] = part

    steps_of(group_rows // chunk, body)
    gradient = total[...] / total_rows
    updated = history[...] + gradient * gradient
    new_history[...] = updated
    new_master[...] = master[...] - step_size * gradient * lax.rsqrt(updated)


def place_kernel(*refs):
    pieces, out = refs[:4], refs[4]
    for place in range(4):
        for g in range(pieces[0].shape[0]):
            out[place_at(place, g)] = pieces[place][g]


def joined(held, other, upper):
    low, high = jnp.where(upper, other, held), jnp.where(upper, held, other)
    return jnp.stack([low, high], axis=1).reshape((2 * held.shape[0],) + held.shape[1:])


def per_device(
    counts, row_totals, column_totals, row_master, row_history, column_master, column_history
):
    size = lax.axis_size("col")
    me = lax.axis_index("col")
    total_rows, block_columns = counts.shape
    all_columns = block_columns * size
    own, width = row_master.shape
    group = size // 4
    group_rows = group * own
    chunk = 128
    terms_type = pltpu.VMEM((2, group, own, block_columns), jnp.float32)

    odd = parity(me)
    last = jnp.where(odd == 1, me >> 1, me >> 2) & 1
    place = (me >> 3) * 2 + last
    top = [size >> k for k in range(1, size.bit_length() - 3)]
    steps = [((bit, bit), (me & bit) != 0) for bit in top] + [(SUM, last != 0)]
    other = first_hop = hop(row_master[None], steps[0][0], size)
    master = lax.optimization_barrier(row_master.astype(jnp.bfloat16))[None]
    for k, (bits, upper) in enumerate(steps):
        if k > 0:
            other = hop(master, bits, size)
        master = joined(master, other.astype(jnp.bfloat16), upper)
    grid = (group // 2, 2, 2, 2, own)
    kept_0, kept_1, sent_0, sent_1, column_copy = pl.pallas_call(
        prepare_kernel,
        out_shape=(terms_type,) * 4 + (pltpu.VMEM(column_master.shape, jnp.bfloat16),),
        in_specs=[HBM] * 4 + [ANY],
        out_specs=[VMEM] * 5,
        scratch_shapes=[
            pltpu.VMEM(grid + (block_columns,), jnp.int32),
            pltpu.VMEM((1, total_rows), jnp.int32),
            pltpu.VMEM((1, block_columns), jnp.int32),
            pltpu.VMEM(column_master.shape, jnp.float32),
            pltpu.VMEM(grid + (128,), jnp.float32),
            pltpu.SemaphoreType.DMA((4,)),
        ],
        compiler_params=PARAMS,
        cost_estimate=pl.CostEstimate(flops=8 * counts.size, bytes_accessed=4 * counts.size, transcendentals=2 * counts.size),
        name="prepare",
    )(
        far(counts.reshape(grid + (block_columns,))),
        far(row_totals.reshape(1, total_rows)),
        far(column_totals.reshape(1, block_columns)),
        far(column_master),
        first_hop,
    )
    other_columns = hop(column_copy, CORE, size)
    received_0, received_1 = hop(sent_0, CORE, size), hop(sent_1, CORE, size)
    mine = master.reshape(group_rows, width)
    beside = hop(mine, SPLIT, size)

    def gradient_of(rows, kept, received):
        return pl.pallas_call(
            functools.partial(rows_kernel, chunk),
            out_shape=(pltpu.VMEM((group_rows, width), jnp.float32), pltpu.VMEM((group_rows, block_columns), jnp.bfloat16)),
            in_specs=[VMEM] * 5,
            out_specs=[VMEM] * 2,
            compiler_params=PARAMS,
            cost_estimate=pl.CostEstimate(flops=8 * group_rows * block_columns * width, bytes_accessed=0, transcendentals=4 * group_rows * block_columns),
            name="rows",
        )(*[near(v) for v in (rows, kept, received, column_copy, other_columns)])

    part_early, slopes_0 = gradient_of(mine, kept_0, received_0)
    part_late, slopes_1 = gradient_of(beside, kept_1, received_1)
    own_rows, part_late = lax.optimization_barrier((jnp.concatenate([mine, beside]), part_late))
    others = hop(own_rows, CORE, size)

    part = part_early + hop(part_late.astype(jnp.bfloat16), SPLIT, size).astype(jnp.float32)
    history = row_history.astype(jnp.bfloat16)[None]
    for bits, upper in steps:
        rounded = part.astype(jnp.bfloat16)
        other = hop(jnp.concatenate([rounded, history.reshape(-1, width)]), bits, size)
        part = rounded.astype(jnp.float32) + other[:group_rows].astype(jnp.float32)
        history = joined(history, other[group_rows:].reshape(history.shape), upper)

    struct = jax.ShapeDtypeStruct(column_master.shape, jnp.float32)
    new_columns, new_column_history = pl.pallas_call(
        functools.partial(columns_kernel, total_rows, chunk),
        out_shape=(struct, struct),
        in_specs=[VMEM] * 10,
        out_specs=[VMEM] * 2,
        scratch_shapes=[pltpu.VMEM(column_master.shape, jnp.float32)],
        compiler_params=PARAMS,
        cost_estimate=pl.CostEstimate(flops=2 * total_rows * block_columns * width, bytes_accessed=4 * column_master.size * 4, transcendentals=0),
        name="columns",
    )(*[near(v) for v in (column_master, column_history, column_copy, sent_0, sent_1, mine, beside, others, slopes_0, slopes_1)])

    def adagrad(master, history, gradient):
        updated = history + gradient * gradient
        return master - step_size * gradient * lax.rsqrt(updated), updated

    gradient = part.reshape(group, own, width) / all_columns
    own_gradient = lax.dynamic_index_in_dim(gradient, place, 0, keepdims=False)
    new_rows, new_row_history = adagrad(row_master, row_history, own_gradient)
    copy = adagrad(master.astype(jnp.float32), history.astype(jnp.float32), gradient)[0].astype(jnp.bfloat16)
    copy, new_columns = lax.optimization_barrier((copy, new_columns))
    beside = hop(copy, SPLIT, size)
    grid_rows = pl.pallas_call(
        place_kernel,
        out_shape=jax.ShapeDtypeStruct(grid + (width,), jnp.bfloat16),
        in_specs=[VMEM] * 4,
        out_specs=VMEM,
        compiler_params=PARAMS,
        name="place",
    )(near(copy), near(beside), near(hop(copy, CORE, size)), near(hop(beside, CORE, size)))
    return (grid_rows.reshape(total_rows, width), new_rows, new_row_history, new_columns, new_column_history)


def solution(mesh):
    return jax.shard_map(
        per_device,
        mesh=mesh,
        in_specs=(
            P("parts", "col"),
            P("parts"),
            P(("parts", "col")),
            P(("parts", "col"), None),
            P(("parts", "col"), None),
            P(("parts", "col"), None),
            P(("parts", "col"), None),
        ),
        out_specs=(
            P("parts", None),
            P(("parts", "col"), None),
            P(("parts", "col"), None),
            P(("parts", "col"), None),
            P(("parts", "col"), None),
        ),
        check_vma=False,
    )
```

```python
import functools

import jax
import jax.numpy as jnp
from jax import lax
from jax.experimental import pallas as pl
from jax.experimental.pallas import tpu as pltpu
from jax.sharding import PartitionSpec as P

step_size = 2.0
VMEM = pl.BlockSpec(memory_space=pltpu.VMEM)
HBM = pl.BlockSpec(memory_space=pltpu.HBM)
ANY = pl.BlockSpec(memory_space=pl.ANY)
PARAMS = pltpu.CompilerParams(vmem_limit_bytes=20 * 1024 * 1024)


def parity(value):
    for shift in (8, 4, 2, 1):
        value = value ^ (value >> shift)
    return value & 1


def hop(value, bits, size):
    pairs = [(i, i ^ (bits[parity(i)] | 1)) for i in range(size)]
    return lax.ppermute(value, "col", pairs)


CORE, SPLIT, SUM = (1, 1), (2, 4), (4, 2)


def near(value):
    return pltpu.with_memory_space_constraint(value, pltpu.VMEM)


def far(value):
    return pltpu.with_memory_space_constraint(value, pltpu.HBM)


def place_at(place, g):
    me = lax.axis_index("col")
    odd = parity(me) ^ (place >> 1)
    one, two = (me >> 1) & 1, (me >> 2) & 1
    split, last, rest = (one + odd * (two - one)) ^ (place & 1), g & 1, g >> 1
    bit_one, bit_two = split + odd * (last - split), last + odd * (split - last)
    return rest, bit_two, bit_one, odd ^ bit_one ^ bit_two ^ parity(rest)


def steps_of(count, body):
    if count == 1:
        body(0)
    else:
        pl.loop(0, count)(body)


def prepare_kernel(counts, row_totals, column_totals, columns, rows, *refs):
    kept_0, kept_1, sent_0, sent_1, column_copy, row_copy = refs[:6]
    near_counts, near_rows, near_columns, near_copy, row_terms, sems = refs[6:]
    groups = kept_0.shape[1]
    copies = [
        pltpu.make_async_copy(row_totals, near_rows, sems.at[0]),
        pltpu.make_async_copy(column_totals, near_columns, sems.at[1]),
        pltpu.make_async_copy(counts, near_counts, sems.at[2]),
        pltpu.make_async_copy(columns, near_copy, sems.at[3]),
        pltpu.make_async_copy(rows, row_copy, sems.at[4]),
    ]
    for copy in copies:
        copy.start()
    copies[0].wait()
    row_floats = near_rows[...].astype(jnp.float32)
    terms = jnp.log(jnp.sum(row_floats, axis=1, keepdims=True)) - jnp.log(row_floats)
    row_terms[...] = jnp.broadcast_to(terms, (128, terms.shape[1])).T.reshape(row_terms.shape)
    copies[1].wait()
    column_term = jnp.log(near_columns[...].astype(jnp.float32))
    copies[2].wait()
    for place in range(4):

        def body(g, place=place):
            at = place_at(place, g)
            amounts = near_counts[at].astype(jnp.float32)
            term = row_terms[at]
            term = jnp.concatenate([term] * (amounts.shape[1] // 128), axis=1)
            target = (kept_0, kept_1, sent_0, sent_1)[place]
            target[0, g] = jnp.log(jnp.maximum(amounts, 1.0)) + (term - column_term)
            target[1, g] = jnp.where(amounts > 0, 0.1 + 0.25 * jnp.sqrt(amounts), 0.0)

        if groups <= 4:
            for g in range(groups):
                body(g)
        else:
            pl.loop(0, groups)(body)
    copies[3].wait()
    column_copy[...] = near_copy[...].astype(jnp.bfloat16)
    copies[4].wait()


def slopes_of(rows, columns, terms, step, chunk):
    group = chunk // terms.shape[2]
    at = pl.ds(step * group, group)
    scores = lax.dot_general(rows, columns, (((1,), (1,)), ((), ())), preferred_element_type=jnp.float32)
    gap = scores - terms[0, at].reshape(scores.shape)
    confidence = terms[1, at].reshape(scores.shape)
    return jnp.where(confidence > 0, confidence * gap, jax.nn.sigmoid(gap)).astype(jnp.bfloat16)


def rows_kernel(chunk, rows, kept, received, columns, other_columns, *refs):
    gradient, slopes = refs[-2:]

    def body(step):
        at = pl.ds(pl.multiple_of(step * chunk, chunk), chunk)
        own = slopes_of(rows[at, :], columns[...], kept, step, chunk)
        slopes[at, :] = own
        gradient[at, :] = jnp.dot(own, columns[...], preferred_element_type=jnp.float32)
        other = slopes_of(rows[at, :], other_columns[...], received, step, chunk)
        gradient[at, :] += jnp.dot(other, other_columns[...], preferred_element_type=jnp.float32)

    steps_of(rows.shape[0] // chunk, body)


def columns_kernel(total_rows, chunk, master, history, columns, sent_0, sent_1, mine, beside, others, slopes_0, slopes_1, *outs):
    new_master, new_history, total = outs
    group_rows = mine.shape[0]
    total[...] = jnp.zeros_like(total)

    def body(step):
        first = pl.multiple_of(step * chunk, chunk)
        at = pl.ds(first, chunk)
        part = total[...]
        for place in range(2):
            rows = (mine, beside)[place][at, :]
            own = (slopes_0, slopes_1)[place][at, :]
            part += lax.dot_general(own, rows, (((0,), (0,)), ((), ())), preferred_element_type=jnp.float32)
            rows = others[pl.ds(place * group_rows + first, chunk), :]
            own = slopes_of(rows, columns[...], (sent_0, sent_1)[place], step, chunk)
            part += lax.dot_general(own, rows, (((0,), (0,)), ((), ())), preferred_element_type=jnp.float32)
        total[...] = part

    steps_of(group_rows // chunk, body)
    gradient = total[...] / total_rows
    updated = history[...] + gradient * gradient
    new_history[...] = updated
    new_master[...] = master[...] - step_size * gradient * lax.rsqrt(updated)


def place_kernel(*refs):
    pieces, out = refs[:4], refs[4]
    for place in range(4):
        for g in range(pieces[0].shape[0]):
            out[place_at(place, g)] = pieces[place][g]


def joined(held, other, upper):
    low, high = jnp.where(upper, other, held), jnp.where(upper, held, other)
    return jnp.stack([low, high], axis=1).reshape((2 * held.shape[0],) + held.shape[1:])


def per_device(
    counts, row_totals, column_totals, row_master, row_history, column_master, column_history
):
    size = lax.axis_size("col")
    me = lax.axis_index("col")
    total_rows, block_columns = counts.shape
    all_columns = block_columns * size
    own, width = row_master.shape
    group = size // 4
    group_rows = group * own
    chunk = 128
    terms_type = pltpu.VMEM((2, group, own, block_columns), jnp.float32)

    odd = parity(me)
    last = jnp.where(odd == 1, me >> 1, me >> 2) & 1
    place = (me >> 3) * 2 + last
    top = [size >> k for k in range(1, size.bit_length() - 3)]
    steps = [((bit, bit), (me & bit) != 0) for bit in top] + [(SUM, last != 0)]
    grid = (group // 2, 2, 2, 2, own)
    kept_0, kept_1, sent_0, sent_1, column_copy, row_copy = pl.pallas_call(
        prepare_kernel,
        out_shape=(terms_type,) * 4 + (pltpu.VMEM(column_master.shape, jnp.bfloat16), pltpu.VMEM(row_master.shape, jnp.float32)),
        in_specs=[HBM] * 5,
        out_specs=[VMEM] * 6,
        scratch_shapes=[
            pltpu.VMEM(grid + (block_columns,), jnp.int32),
            pltpu.VMEM((1, total_rows), jnp.int32),
            pltpu.VMEM((1, block_columns), jnp.int32),
            pltpu.VMEM(column_master.shape, jnp.float32),
            pltpu.VMEM(grid + (128,), jnp.float32),
            pltpu.SemaphoreType.DMA((5,)),
        ],
        compiler_params=PARAMS,
        cost_estimate=pl.CostEstimate(flops=8 * counts.size, bytes_accessed=4 * counts.size, transcendentals=2 * counts.size),
        name="prepare",
    )(
        far(counts.reshape(grid + (block_columns,))),
        far(row_totals.reshape(1, total_rows)),
        far(column_totals.reshape(1, block_columns)),
        far(column_master),
        far(row_master),
    )
    other_columns = hop(column_copy, CORE, size)
    received_0, received_1 = hop(sent_0, CORE, size), hop(sent_1, CORE, size)
    first_hop = hop(row_master[None], steps[0][0], size)
    master, other = row_copy[None], first_hop
    for k, (bits, upper) in enumerate(steps):
        if k > 0:
            other = hop(master, bits, size)
        master = joined(master, other, upper).astype(jnp.bfloat16)
    mine = master.reshape(group_rows, width)
    beside = hop(mine, SPLIT, size)

    def gradient_of(rows, kept, received, *after):
        return pl.pallas_call(
            functools.partial(rows_kernel, chunk),
            out_shape=(pltpu.VMEM((group_rows, width), jnp.float32), pltpu.VMEM((group_rows, block_columns), jnp.bfloat16)),
            in_specs=[VMEM] * 5 + [ANY] * len(after),
            out_specs=[VMEM] * 2,
            compiler_params=PARAMS,
            cost_estimate=pl.CostEstimate(flops=8 * group_rows * block_columns * width, bytes_accessed=0, transcendentals=4 * group_rows * block_columns),
            name="rows",
        )(*[near(v) for v in (rows, kept, received, column_copy, other_columns)], *after)

    part_early, slopes_0 = gradient_of(mine, kept_0, received_0, first_hop)
    part_late, slopes_1 = gradient_of(beside, kept_1, received_1)
    own_rows, part_late = lax.optimization_barrier((jnp.concatenate([mine, beside]), part_late))
    others = hop(own_rows, CORE, size)

    part = part_early + hop(part_late.astype(jnp.bfloat16), SPLIT, size).astype(jnp.float32)
    history = row_history.astype(jnp.bfloat16)[None]
    for bits, upper in steps:
        rounded = part.astype(jnp.bfloat16)
        other = hop(jnp.concatenate([rounded, history.reshape(-1, width)]), bits, size)
        part = rounded.astype(jnp.float32) + other[:group_rows].astype(jnp.float32)
        history = joined(history, other[group_rows:].reshape(history.shape), upper)

    struct = jax.ShapeDtypeStruct(column_master.shape, jnp.float32)
    new_columns, new_column_history = pl.pallas_call(
        functools.partial(columns_kernel, total_rows, chunk),
        out_shape=(struct, struct),
        in_specs=[VMEM] * 10,
        out_specs=[VMEM] * 2,
        scratch_shapes=[pltpu.VMEM(column_master.shape, jnp.float32)],
        compiler_params=PARAMS,
        cost_estimate=pl.CostEstimate(flops=2 * total_rows * block_columns * width, bytes_accessed=4 * column_master.size * 4, transcendentals=0),
        name="columns",
    )(*[near(v) for v in (column_master, column_history, column_copy, sent_0, sent_1, mine, beside, others, slopes_0, slopes_1)])

    def adagrad(master, history, gradient):
        updated = history + gradient * gradient
        return master - step_size * gradient * lax.rsqrt(updated), updated

    gradient = part.reshape(group, own, width) / all_columns
    own_gradient = lax.dynamic_index_in_dim(gradient, place, 0, keepdims=False)
    new_rows, new_row_history = adagrad(row_master, row_history, own_gradient)
    copy = adagrad(master.astype(jnp.float32), history.astype(jnp.float32), gradient)[0].astype(jnp.bfloat16)
    copy, new_columns = lax.optimization_barrier((copy, new_columns))
    beside = hop(copy, SPLIT, size)
    grid_rows = pl.pallas_call(
        place_kernel,
        out_shape=jax.ShapeDtypeStruct(grid + (width,), jnp.bfloat16),
        in_specs=[VMEM] * 4,
        out_specs=VMEM,
        compiler_params=PARAMS,
        name="place",
    )(near(copy), near(beside), near(hop(copy, CORE, size)), near(hop(beside, CORE, size)))
    return (grid_rows.reshape(total_rows, width), new_rows, new_row_history, new_columns, new_column_history)


def solution(mesh):
    return jax.shard_map(
        per_device,
        mesh=mesh,
        in_specs=(
            P("parts", "col"),
            P("parts"),
            P(("parts", "col")),
            P(("parts", "col"), None),
            P(("parts", "col"), None),
            P(("parts", "col"), None),
            P(("parts", "col"), None),
        ),
        out_specs=(
            P("parts", None),
            P(("parts", "col"), None),
            P(("parts", "col"), None),
            P(("parts", "col"), None),
            P(("parts", "col"), None),
        ),
        check_vma=False,
    )
```

```python
import functools

import jax
import jax.numpy as jnp
from jax import lax
from jax.experimental import pallas as pl
from jax.experimental.pallas import tpu as pltpu
from jax.sharding import PartitionSpec as P

step_size = 2.0
VMEM = pl.BlockSpec(memory_space=pltpu.VMEM)
HBM = pl.BlockSpec(memory_space=pltpu.HBM)
ANY = pl.BlockSpec(memory_space=pl.ANY)
PARAMS = pltpu.CompilerParams(vmem_limit_bytes=20 * 1024 * 1024)


def parity(value):
    for shift in (4, 2, 1):
        value = value ^ (value >> shift)
    return value & 1


def top_bits(size):
    return [size >> k for k in range(1, size.bit_length() - 3)]


def last_bit(me):
    return ((me >> 2) ^ (parity(me) & ((me >> 1) ^ (me >> 2)))) & 1


def hop(value, bits, size):
    pairs = [(i, i ^ (bits[parity(i)] | 1)) for i in range(size)]
    return lax.ppermute(value, "col", pairs)


CORE, SPLIT, SUM = (1, 1), (2, 4), (4, 2)


def near(value):
    return pltpu.with_memory_space_constraint(value, pltpu.VMEM)


def far(value):
    return pltpu.with_memory_space_constraint(value, pltpu.HBM)


def place_at(place, g):
    me = lax.axis_index("col")
    odd = parity(me) ^ (place >> 1)
    one, two = (me >> 1) & 1, (me >> 2) & 1
    split, last, rest = (one + odd * (two - one)) ^ (place & 1), g & 1, g >> 1
    bit_one, bit_two = split + odd * (last - split), last + odd * (split - last)
    return rest, bit_two, bit_one, odd ^ bit_one ^ bit_two ^ parity(rest)


def steps_of(count, body):
    if count == 1:
        body(0)
    else:
        pl.loop(0, count)(body)


def prepare_kernel(counts, row_totals, column_totals, columns, rows, history, *refs):
    kept_0, kept_1, sent_0, sent_1, column_copy, row_copy, history_copy, upper = refs[:8]
    near_counts, near_rows, near_columns, near_copy, near_history, row_terms, sems = refs[8:]
    groups = kept_0.shape[1]
    copies = [
        pltpu.make_async_copy(row_totals, near_rows, sems.at[0]),
        pltpu.make_async_copy(column_totals, near_columns, sems.at[1]),
        pltpu.make_async_copy(counts, near_counts, sems.at[2]),
        pltpu.make_async_copy(columns, near_copy, sems.at[3]),
        pltpu.make_async_copy(rows, row_copy, sems.at[4]),
        pltpu.make_async_copy(history, near_history, sems.at[5]),
    ]
    for copy in copies:
        copy.start()
    me = lax.axis_index("col")
    changed = [(me // bit) & 1 for bit in top_bits(8 * counts.shape[0])] + [last_bit(me)]
    step = lax.broadcasted_iota(jnp.int32, upper.shape, 0)
    upper[...] = sum(jnp.where(step == k, bit, 0) for k, bit in enumerate(changed)).astype(jnp.float32)
    copies[0].wait()
    row_floats = near_rows[...].astype(jnp.float32)
    terms = jnp.log(jnp.sum(row_floats, axis=1, keepdims=True)) - jnp.log(row_floats)
    row_terms[...] = jnp.broadcast_to(terms, (128, terms.shape[1])).T.reshape(row_terms.shape)
    copies[1].wait()
    column_term = jnp.log(near_columns[...].astype(jnp.float32))
    copies[2].wait()
    for place in range(4):

        def body(g, place=place):
            at = place_at(place, g)
            amounts = near_counts[at].astype(jnp.float32)
            term = row_terms[at]
            term = jnp.concatenate([term] * (amounts.shape[1] // 128), axis=1)
            target = (kept_0, kept_1, sent_0, sent_1)[place]
            target[0, g] = jnp.log(jnp.maximum(amounts, 1.0)) + (term - column_term)
            target[1, g] = jnp.where(amounts > 0, 0.1 + 0.25 * jnp.sqrt(amounts), 0.0)

        if groups <= 4:
            for g in range(groups):
                body(g)
        else:
            pl.loop(0, groups)(body)
    copies[3].wait()
    column_copy[...] = near_copy[...].astype(jnp.bfloat16)
    copies[4].wait()
    copies[5].wait()
    history_copy[...] = near_history[...].astype(jnp.bfloat16)


def slopes_of(rows, columns, terms, step, chunk):
    group = chunk // terms.shape[2]
    at = pl.ds(step * group, group)
    scores = lax.dot_general(rows, columns, (((1,), (1,)), ((), ())), preferred_element_type=jnp.float32)
    gap = scores - terms[0, at].reshape(scores.shape)
    confidence = terms[1, at].reshape(scores.shape)
    return jnp.where(confidence > 0, confidence * gap, jax.nn.sigmoid(gap)).astype(jnp.bfloat16)


def rows_kernel(chunk, rows, kept, received, columns, other_columns, *refs):
    gradient, slopes = refs[-2:]

    def body(step):
        at = pl.ds(pl.multiple_of(step * chunk, chunk), chunk)
        own = slopes_of(rows[at, :], columns[...], kept, step, chunk)
        slopes[at, :] = own
        gradient[at, :] = jnp.dot(own, columns[...], preferred_element_type=jnp.float32)
        other = slopes_of(rows[at, :], other_columns[...], received, step, chunk)
        gradient[at, :] += jnp.dot(other, other_columns[...], preferred_element_type=jnp.float32)

    steps_of(rows.shape[0] // chunk, body)


def columns_kernel(total_rows, chunk, master, history, columns, sent_0, sent_1, mine, beside, others, slopes_0, slopes_1, *outs):
    new_master, new_history, total = outs
    group_rows = mine.shape[0]
    total[...] = jnp.zeros_like(total)

    def body(step):
        first = pl.multiple_of(step * chunk, chunk)
        at = pl.ds(first, chunk)
        part = total[...]
        for place in range(2):
            rows = (mine, beside)[place][at, :]
            own = (slopes_0, slopes_1)[place][at, :]
            part += lax.dot_general(own, rows, (((0,), (0,)), ((), ())), preferred_element_type=jnp.float32)
            rows = others[pl.ds(place * group_rows + first, chunk), :]
            own = slopes_of(rows, columns[...], (sent_0, sent_1)[place], step, chunk)
            part += lax.dot_general(own, rows, (((0,), (0,)), ((), ())), preferred_element_type=jnp.float32)
        total[...] = part

    steps_of(group_rows // chunk, body)
    gradient = total[...] / total_rows
    updated = history[...] + gradient * gradient
    new_history[...] = updated
    new_master[...] = master[...] - step_size * gradient * lax.rsqrt(updated)


def place_kernel(*refs):
    pieces, out = refs[:4], refs[4]
    for place in range(4):
        for g in range(pieces[0].shape[0]):
            out[place_at(place, g)] = pieces[place][g]


def joined(held, other, upper):
    low, high = jnp.where(upper, other, held), jnp.where(upper, held, other)
    return jnp.stack([low, high], axis=1).reshape((2 * held.shape[0],) + held.shape[1:])


def per_device(
    counts, row_totals, column_totals, row_master, row_history, column_master, column_history
):
    size = lax.axis_size("col")
    me = lax.axis_index("col")
    total_rows, block_columns = counts.shape
    all_columns = block_columns * size
    own, width = row_master.shape
    group = size // 4
    group_rows = group * own
    chunk = 128
    terms_type = pltpu.VMEM((2, group, own, block_columns), jnp.float32)

    grid = (group // 2, 2, 2, 2, own)
    kept_0, kept_1, sent_0, sent_1, column_copy, row_copy, history, side = pl.pallas_call(
        prepare_kernel,
        out_shape=(terms_type,) * 4 + (pltpu.VMEM(column_master.shape, jnp.bfloat16), pltpu.VMEM(row_master.shape, jnp.float32), pltpu.VMEM(row_master.shape, jnp.bfloat16), pltpu.VMEM((8, width), jnp.float32)),
        in_specs=[HBM] * 6,
        out_specs=[VMEM] * 8,
        scratch_shapes=[
            pltpu.VMEM(grid + (block_columns,), jnp.int32),
            pltpu.VMEM((1, total_rows), jnp.int32),
            pltpu.VMEM((1, block_columns), jnp.int32),
            pltpu.VMEM(column_master.shape, jnp.float32),
            pltpu.VMEM(row_history.shape, jnp.float32),
            pltpu.VMEM(grid + (128,), jnp.float32),
            pltpu.SemaphoreType.DMA((6,)),
        ],
        compiler_params=PARAMS,
        cost_estimate=pl.CostEstimate(flops=8 * counts.size, bytes_accessed=4 * counts.size, transcendentals=2 * counts.size),
        name="prepare",
    )(
        far(counts.reshape(grid + (block_columns,))),
        far(row_totals.reshape(1, total_rows)),
        far(column_totals.reshape(1, block_columns)),
        far(column_master),
        far(row_master),
        far(row_history),
    )
    other_columns = hop(column_copy, CORE, size)
    received_0, received_1 = hop(sent_0, CORE, size), hop(sent_1, CORE, size)
    steps = [((bit, bit), side[k] > 0) for k, bit in enumerate(top_bits(size))]
    steps.append((SUM, side[len(steps)] > 0))
    first_hop = hop(row_master[None], steps[0][0], size)
    master, other = row_copy[None], first_hop
    for k, (bits, upper) in enumerate(steps):
        if k > 0:
            other = hop(master, bits, size)
        master = joined(master, other, upper).astype(jnp.bfloat16)
    mine = master.reshape(group_rows, width)
    beside = hop(mine, SPLIT, size)
    def gradient_of(rows, kept, received, *after):
        return pl.pallas_call(
            functools.partial(rows_kernel, chunk),
            out_shape=(pltpu.VMEM((group_rows, width), jnp.float32), pltpu.VMEM((group_rows, block_columns), jnp.bfloat16)),
            in_specs=[VMEM] * 5 + [ANY] * len(after),
            out_specs=[VMEM] * 2,
            compiler_params=PARAMS,
            cost_estimate=pl.CostEstimate(flops=8 * group_rows * block_columns * width, bytes_accessed=0, transcendentals=4 * group_rows * block_columns),
            name="rows",
        )(*[near(v) for v in (rows, kept, received, column_copy, other_columns)], *after)

    part_early, slopes_0 = gradient_of(mine, kept_0, received_0, first_hop)
    history, part_early = lax.optimization_barrier((history[None], part_early))
    for bits, upper in steps[:-1]:
        history = joined(history, hop(history, bits, size), upper)
    part_late, slopes_1 = gradient_of(beside, kept_1, received_1)
    own_rows, part_late = lax.optimization_barrier((jnp.concatenate([mine, beside]), part_late))
    others = hop(own_rows, CORE, size)

    part = part_early + hop(part_late.astype(jnp.bfloat16), SPLIT, size).astype(jnp.float32)
    struct = jax.ShapeDtypeStruct(column_master.shape, jnp.float32)
    new_columns, new_column_history = pl.pallas_call(
        functools.partial(columns_kernel, total_rows, chunk),
        out_shape=(struct, struct),
        in_specs=[VMEM] * 10,
        out_specs=[VMEM] * 2,
        scratch_shapes=[pltpu.VMEM(column_master.shape, jnp.float32)],
        compiler_params=PARAMS,
        cost_estimate=pl.CostEstimate(flops=2 * total_rows * block_columns * width, bytes_accessed=4 * column_master.size * 4, transcendentals=0),
        name="columns",
    )(*[near(v) for v in (column_master, column_history, column_copy, sent_0, sent_1, mine, beside, others, slopes_0, slopes_1)])

    history, new_columns = lax.optimization_barrier((history, new_columns))
    last_history = hop(history, SUM, size)
    for bits, upper in steps:
        rounded = part.astype(jnp.bfloat16)
        part = rounded.astype(jnp.float32) + hop(rounded, bits, size).astype(jnp.float32)
    history = joined(history, last_history, steps[-1][1])

    def adagrad(master, history, gradient):
        updated = history + gradient * gradient
        return master - step_size * gradient * lax.rsqrt(updated), updated

    gradient = part.reshape(group, own, width) / all_columns
    own_gradient = lax.dynamic_index_in_dim(gradient, (me >> 3) * 2 + last_bit(me), 0, keepdims=False)
    new_rows, new_row_history = adagrad(row_master, row_history, own_gradient)
    copy = adagrad(master.astype(jnp.float32), history.astype(jnp.float32), gradient)[0].astype(jnp.bfloat16)
    beside = hop(copy, SPLIT, size)
    grid_rows = pl.pallas_call(
        place_kernel,
        out_shape=jax.ShapeDtypeStruct(grid + (width,), jnp.bfloat16),
        in_specs=[VMEM] * 4,
        out_specs=VMEM,
        compiler_params=PARAMS,
        name="place",
    )(near(copy), near(beside), near(hop(copy, CORE, size)), near(hop(beside, CORE, size)))
    return (grid_rows.reshape(total_rows, width), new_rows, new_row_history, new_columns, new_column_history)


def solution(mesh):
    return jax.shard_map(
        per_device,
        mesh=mesh,
        in_specs=(
            P("parts", "col"),
            P("parts"),
            P(("parts", "col")),
            P(("parts", "col"), None),
            P(("parts", "col"), None),
            P(("parts", "col"), None),
            P(("parts", "col"), None),
        ),
        out_specs=(
            P("parts", None),
            P(("parts", "col"), None),
            P(("parts", "col"), None),
            P(("parts", "col"), None),
            P(("parts", "col"), None),
        ),
        check_vma=False,
    )
```

```python
import functools

import jax
import jax.numpy as jnp
from jax import lax
from jax.experimental import pallas as pl
from jax.experimental.pallas import tpu as pltpu
from jax.sharding import PartitionSpec as P

step_size = 2.0
VMEM = pl.BlockSpec(memory_space=pltpu.VMEM)
HBM = pl.BlockSpec(memory_space=pltpu.HBM)
ANY = pl.BlockSpec(memory_space=pl.ANY)
PARAMS = pltpu.CompilerParams(vmem_limit_bytes=20 * 1024 * 1024)


def parity(value):
    for shift in (4, 2, 1):
        value = value ^ (value >> shift)
    return value & 1


def top_bits(size):
    return [size >> k for k in range(1, size.bit_length() - 3)]


def last_bit(me):
    return ((me >> 2) ^ (parity(me) & ((me >> 1) ^ (me >> 2)))) & 1


def hop(value, bits, size):
    pairs = [(i, i ^ (bits[parity(i)] | 1)) for i in range(size)]
    return lax.ppermute(value, "col", pairs)


CORE, SPLIT, SUM = (1, 1), (2, 4), (4, 2)


def near(value):
    return pltpu.with_memory_space_constraint(value, pltpu.VMEM)


def far(value):
    return pltpu.with_memory_space_constraint(value, pltpu.HBM)


def place_at(place, g):
    me = lax.axis_index("col")
    odd = parity(me) ^ (place >> 1)
    one, two = (me >> 1) & 1, (me >> 2) & 1
    split, last, rest = (one + odd * (two - one)) ^ (place & 1), g & 1, g >> 1
    bit_one, bit_two = split + odd * (last - split), last + odd * (split - last)
    return rest, bit_two, bit_one, odd ^ bit_one ^ bit_two ^ parity(rest)


def steps_of(count, body):
    if count == 1:
        body(0)
    else:
        pl.loop(0, count)(body)


def prepare_kernel(counts, row_totals, column_totals, columns, rows, history, *refs):
    kept_0, kept_1, sent_0, sent_1, column_copy, row_copy, history_copy, upper = refs[:8]
    near_counts, near_rows, near_columns, near_copy, near_history, row_terms, sems = refs[8:]
    groups = kept_0.shape[1]
    copies = [
        pltpu.make_async_copy(row_totals, near_rows, sems.at[0]),
        pltpu.make_async_copy(column_totals, near_columns, sems.at[1]),
        pltpu.make_async_copy(counts, near_counts, sems.at[2]),
        pltpu.make_async_copy(columns, near_copy, sems.at[3]),
        pltpu.make_async_copy(rows, row_copy, sems.at[4]),
        pltpu.make_async_copy(history, near_history, sems.at[5]),
    ]
    for copy in copies:
        copy.start()
    me = lax.axis_index("col")
    changed = [(me // bit) & 1 for bit in top_bits(8 * counts.shape[0])] + [last_bit(me)]
    step = lax.broadcasted_iota(jnp.int32, upper.shape, 0)
    upper[...] = sum(jnp.where(step == k, bit, 0) for k, bit in enumerate(changed)).astype(jnp.float32)
    copies[0].wait()
    row_floats = near_rows[...].astype(jnp.float32)
    terms = jnp.log(jnp.sum(row_floats, axis=1, keepdims=True)) - jnp.log(row_floats)
    row_terms[...] = jnp.broadcast_to(terms, (128, terms.shape[1])).T.reshape(row_terms.shape)
    copies[1].wait()
    column_term = jnp.log(near_columns[...].astype(jnp.float32))
    copies[2].wait()
    for place in range(4):

        def body(g, place=place):
            at = place_at(place, g)
            amounts = near_counts[at].astype(jnp.float32)
            term = row_terms[at]
            term = jnp.concatenate([term] * (amounts.shape[1] // 128), axis=1)
            target = (kept_0, kept_1, sent_0, sent_1)[place]
            target[0, g] = jnp.log(jnp.maximum(amounts, 1.0)) + (term - column_term)
            target[1, g] = jnp.where(amounts > 0, 0.1 + 0.25 * jnp.sqrt(amounts), 0.0)

        if groups <= 4:
            for g in range(groups):
                body(g)
        else:
            pl.loop(0, groups)(body)
    copies[3].wait()
    column_copy[...] = near_copy[...].astype(jnp.bfloat16)
    copies[4].wait()
    copies[5].wait()
    history_copy[...] = near_history[...].astype(jnp.bfloat16)


def slopes_of(rows, columns, terms, step, chunk):
    group = chunk // terms.shape[2]
    at = pl.ds(step * group, group)
    scores = lax.dot_general(rows, columns, (((1,), (1,)), ((), ())), preferred_element_type=jnp.float32)
    gap = scores - terms[0, at].reshape(scores.shape)
    confidence = terms[1, at].reshape(scores.shape)
    return jnp.where(confidence > 0, confidence * gap, jax.nn.sigmoid(gap)).astype(jnp.bfloat16)


def rows_kernel(chunk, rows, kept, received, columns, other_columns, *refs):
    gradient, slopes = refs[-2:]

    def body(step):
        at = pl.ds(pl.multiple_of(step * chunk, chunk), chunk)
        own = slopes_of(rows[at, :], columns[...], kept, step, chunk)
        slopes[at, :] = own
        gradient[at, :] = jnp.dot(own, columns[...], preferred_element_type=jnp.float32)
        other = slopes_of(rows[at, :], other_columns[...], received, step, chunk)
        gradient[at, :] += jnp.dot(other, other_columns[...], preferred_element_type=jnp.float32)

    steps_of(rows.shape[0] // chunk, body)


def columns_kernel(total_rows, chunk, master, history, columns, sent_0, sent_1, mine, beside, others, slopes_0, slopes_1, *outs):
    new_master, new_history, total = outs
    group_rows = mine.shape[0]
    total[...] = jnp.zeros_like(total)

    def body(step):
        first = pl.multiple_of(step * chunk, chunk)
        at = pl.ds(first, chunk)
        part = total[...]
        for place in range(2):
            rows = (mine, beside)[place][at, :]
            own = (slopes_0, slopes_1)[place][at, :]
            part += lax.dot_general(own, rows, (((0,), (0,)), ((), ())), preferred_element_type=jnp.float32)
            rows = others[pl.ds(place * group_rows + first, chunk), :]
            own = slopes_of(rows, columns[...], (sent_0, sent_1)[place], step, chunk)
            part += lax.dot_general(own, rows, (((0,), (0,)), ((), ())), preferred_element_type=jnp.float32)
        total[...] = part

    steps_of(group_rows // chunk, body)
    gradient = total[...] / total_rows
    updated = history[...] + gradient * gradient
    new_history[...] = updated
    new_master[...] = master[...] - step_size * gradient * lax.rsqrt(updated)


def place_kernel(*refs):
    pieces, out = refs[:4], refs[4]
    for place in range(4):
        for g in range(pieces[0].shape[0]):
            out[place_at(place, g)] = pieces[place][g]


def joined(held, other, upper):
    low, high = jnp.where(upper, other, held), jnp.where(upper, held, other)
    return jnp.stack([low, high], axis=1).reshape((2 * held.shape[0],) + held.shape[1:])


def per_device(
    counts, row_totals, column_totals, row_master, row_history, column_master, column_history
):
    size = lax.axis_size("col")
    me = lax.axis_index("col")
    total_rows, block_columns = counts.shape
    all_columns = block_columns * size
    own, width = row_master.shape
    group = size // 4
    group_rows = group * own
    chunk = 128
    terms_type = pltpu.VMEM((2, group, own, block_columns), jnp.float32)

    grid = (group // 2, 2, 2, 2, own)
    kept_0, kept_1, sent_0, sent_1, column_copy, row_copy, history, side = pl.pallas_call(
        prepare_kernel,
        out_shape=(terms_type,) * 4 + (pltpu.VMEM(column_master.shape, jnp.bfloat16), pltpu.VMEM(row_master.shape, jnp.float32), pltpu.VMEM(row_master.shape, jnp.bfloat16), pltpu.VMEM((8, width), jnp.float32)),
        in_specs=[HBM] * 6,
        out_specs=[VMEM] * 8,
        scratch_shapes=[
            pltpu.VMEM(grid + (block_columns,), jnp.int32),
            pltpu.VMEM((1, total_rows), jnp.int32),
            pltpu.VMEM((1, block_columns), jnp.int32),
            pltpu.VMEM(column_master.shape, jnp.float32),
            pltpu.VMEM(row_history.shape, jnp.float32),
            pltpu.VMEM(grid + (128,), jnp.float32),
            pltpu.SemaphoreType.DMA((6,)),
        ],
        compiler_params=PARAMS,
        cost_estimate=pl.CostEstimate(flops=8 * counts.size, bytes_accessed=4 * counts.size, transcendentals=2 * counts.size),
        name="prepare",
    )(
        far(counts.reshape(grid + (block_columns,))),
        far(row_totals.reshape(1, total_rows)),
        far(column_totals.reshape(1, block_columns)),
        far(column_master),
        far(row_master),
        far(row_history),
    )
    other_columns = hop(column_copy, CORE, size)
    received_0, received_1 = hop(sent_0, CORE, size), hop(sent_1, CORE, size)
    steps = [((bit, bit), side[k] > 0) for k, bit in enumerate(top_bits(size))]
    steps.append((SUM, side[len(steps)] > 0))
    first_hop = hop(row_master[None], steps[0][0], size)
    master, other = row_copy[None], first_hop
    for k, (bits, upper) in enumerate(steps):
        if k > 0:
            other = hop(master, bits, size)
        master = joined(master, other, upper).astype(jnp.bfloat16)
    mine = master.reshape(group_rows, width)
    beside = hop(mine, SPLIT, size)
    history, _ = lax.optimization_barrier((history[None], mine))
    for bits, upper in steps[:-1]:
        history = joined(history, hop(history, bits, size), upper)

    def gradient_of(rows, kept, received, *after):
        return pl.pallas_call(
            functools.partial(rows_kernel, chunk),
            out_shape=(pltpu.VMEM((group_rows, width), jnp.float32), pltpu.VMEM((group_rows, block_columns), jnp.bfloat16)),
            in_specs=[VMEM] * 5 + [ANY] * len(after),
            out_specs=[VMEM] * 2,
            compiler_params=PARAMS,
            cost_estimate=pl.CostEstimate(flops=8 * group_rows * block_columns * width, bytes_accessed=0, transcendentals=4 * group_rows * block_columns),
            name="rows",
        )(*[near(v) for v in (rows, kept, received, column_copy, other_columns)], *after)

    part_late, slopes_1 = gradient_of(beside, kept_1, received_1)
    part_early, slopes_0 = gradient_of(mine, kept_0, received_0, first_hop)
    own_rows, part_late = lax.optimization_barrier((jnp.concatenate([mine, beside]), part_late))
    others = hop(own_rows, CORE, size)

    part = part_early + hop(part_late.astype(jnp.bfloat16), SPLIT, size).astype(jnp.float32)
    struct = jax.ShapeDtypeStruct(column_master.shape, jnp.float32)
    new_columns, new_column_history = pl.pallas_call(
        functools.partial(columns_kernel, total_rows, chunk),
        out_shape=(struct, struct),
        in_specs=[VMEM] * 10,
        out_specs=[VMEM] * 2,
        scratch_shapes=[pltpu.VMEM(column_master.shape, jnp.float32)],
        compiler_params=PARAMS,
        cost_estimate=pl.CostEstimate(flops=2 * total_rows * block_columns * width, bytes_accessed=4 * column_master.size * 4, transcendentals=0),
        name="columns",
    )(*[near(v) for v in (column_master, column_history, column_copy, sent_0, sent_1, mine, beside, others, slopes_0, slopes_1)])

    history, new_columns = lax.optimization_barrier((history, new_columns))
    last_history = hop(history, SUM, size)
    for bits, upper in steps:
        rounded = part.astype(jnp.bfloat16)
        part = rounded.astype(jnp.float32) + hop(rounded, bits, size).astype(jnp.float32)
    history = joined(history, last_history, steps[-1][1])

    def adagrad(master, history, gradient):
        updated = history + gradient * gradient
        return master - step_size * gradient * lax.rsqrt(updated), updated

    gradient = part.reshape(group, own, width) / all_columns
    own_gradient = lax.dynamic_index_in_dim(gradient, (me >> 3) * 2 + last_bit(me), 0, keepdims=False)
    new_rows, new_row_history = adagrad(row_master, row_history, own_gradient)
    copy = adagrad(master.astype(jnp.float32), history.astype(jnp.float32), gradient)[0].astype(jnp.bfloat16)
    beside = hop(copy, SPLIT, size)
    grid_rows = pl.pallas_call(
        place_kernel,
        out_shape=jax.ShapeDtypeStruct(grid + (width,), jnp.bfloat16),
        in_specs=[VMEM] * 4,
        out_specs=VMEM,
        compiler_params=PARAMS,
        name="place",
    )(near(copy), near(beside), near(hop(copy, CORE, size)), near(hop(beside, CORE, size)))
    return (grid_rows.reshape(total_rows, width), new_rows, new_row_history, new_columns, new_column_history)


def solution(mesh):
    return jax.shard_map(
        per_device,
        mesh=mesh,
        in_specs=(
            P("parts", "col"),
            P("parts"),
            P(("parts", "col")),
            P(("parts", "col"), None),
            P(("parts", "col"), None),
            P(("parts", "col"), None),
            P(("parts", "col"), None),
        ),
        out_specs=(
            P("parts", None),
            P(("parts", "col"), None),
            P(("parts", "col"), None),
            P(("parts", "col"), None),
            P(("parts", "col"), None),
        ),
        check_vma=False,
    )
```

```python
import functools

import jax
import jax.numpy as jnp
from jax import lax
from jax.experimental import pallas as pl
from jax.experimental.pallas import tpu as pltpu
from jax.sharding import PartitionSpec as P

step_size = 2.0
VMEM = pl.BlockSpec(memory_space=pltpu.VMEM)
HBM = pl.BlockSpec(memory_space=pltpu.HBM)
ANY = pl.BlockSpec(memory_space=pl.ANY)
PARAMS = pltpu.CompilerParams(vmem_limit_bytes=20 * 1024 * 1024)


def parity(value):
    for shift in (4, 2, 1):
        value = value ^ (value >> shift)
    return value & 1


def top_bits(size):
    return [size >> k for k in range(1, size.bit_length() - 3)]


def last_bit(me):
    return ((me >> 2) ^ (parity(me) & ((me >> 1) ^ (me >> 2)))) & 1


def hop(value, bits, size):
    pairs = [(i, i ^ (bits[parity(i)] | 1)) for i in range(size)]
    return lax.ppermute(value, "col", pairs)


CORE, SPLIT, SUM = (1, 1), (2, 4), (4, 2)


def near(value):
    return pltpu.with_memory_space_constraint(value, pltpu.VMEM)


def far(value):
    return pltpu.with_memory_space_constraint(value, pltpu.HBM)


def place_at(place, g):
    me = lax.axis_index("col")
    odd = parity(me) ^ (place >> 1)
    one, two = (me >> 1) & 1, (me >> 2) & 1
    split, last, rest = (one + odd * (two - one)) ^ (place & 1), g & 1, g >> 1
    bit_one, bit_two = split + odd * (last - split), last + odd * (split - last)
    return rest, bit_two, bit_one, odd ^ bit_one ^ bit_two ^ parity(rest)


def steps_of(count, body):
    if count == 1:
        body(0)
    else:
        pl.loop(0, count)(body)


def prepare_kernel(counts, row_totals, column_totals, columns, rows, history, *refs):
    kept_0, kept_1, sent_0, sent_1, column_copy, row_copy, history_copy, upper = refs[:8]
    near_counts, near_rows, near_columns, near_copy, near_history, row_terms, sems = refs[8:]
    groups = kept_0.shape[1]
    copies = [
        pltpu.make_async_copy(row_totals, near_rows, sems.at[0]),
        pltpu.make_async_copy(column_totals, near_columns, sems.at[1]),
        pltpu.make_async_copy(counts, near_counts, sems.at[2]),
        pltpu.make_async_copy(columns, near_copy, sems.at[3]),
        pltpu.make_async_copy(rows, row_copy, sems.at[4]),
        pltpu.make_async_copy(history, near_history, sems.at[5]),
    ]
    for copy in copies:
        copy.start()
    me = lax.axis_index("col")
    changed = [(me // bit) & 1 for bit in top_bits(8 * counts.shape[0])] + [last_bit(me)]
    step = lax.broadcasted_iota(jnp.int32, upper.shape, 0)
    upper[...] = sum(jnp.where(step == k, bit, 0) for k, bit in enumerate(changed)).astype(jnp.float32)
    copies[0].wait()
    row_floats = near_rows[...].astype(jnp.float32)
    terms = jnp.log(jnp.sum(row_floats, axis=1, keepdims=True)) - jnp.log(row_floats)
    row_terms[...] = jnp.broadcast_to(terms, (128, terms.shape[1])).T.reshape(row_terms.shape)
    copies[1].wait()
    column_term = jnp.log(near_columns[...].astype(jnp.float32))
    copies[2].wait()
    for place in range(4):

        def body(g, place=place):
            at = place_at(place, g)
            amounts = near_counts[at].astype(jnp.float32)
            term = row_terms[at]
            term = jnp.concatenate([term] * (amounts.shape[1] // 128), axis=1)
            target = (kept_0, kept_1, sent_0, sent_1)[place]
            target[0, g] = jnp.log(jnp.maximum(amounts, 1.0)) + (term - column_term)
            target[1, g] = jnp.where(amounts > 0, 0.1 + 0.25 * jnp.sqrt(amounts), 0.0)

        if groups <= 4:
            for g in range(groups):
                body(g)
        else:
            pl.loop(0, groups)(body)
    copies[3].wait()
    column_copy[...] = near_copy[...].astype(jnp.bfloat16)
    copies[4].wait()
    copies[5].wait()
    history_copy[...] = near_history[...].astype(jnp.bfloat16)


def slopes_of(rows, columns, terms, step, chunk, at_columns=slice(None)):
    group = chunk // terms.shape[2]
    at = pl.ds(step * group, group)
    scores = lax.dot_general(rows, columns, (((1,), (1,)), ((), ())), preferred_element_type=jnp.float32)
    gap = scores - terms[0, at, :, at_columns].reshape(scores.shape)
    confidence = terms[1, at, :, at_columns].reshape(scores.shape)
    return jnp.where(confidence > 0, confidence * gap, jax.nn.sigmoid(gap)).astype(jnp.bfloat16)


def rows_kernel(chunk, rows, kept, received, columns, other_columns, *refs):
    gradient, slopes = refs[-2:]
    half = columns.shape[0] // 2

    def body(step):
        at = pl.ds(pl.multiple_of(step * chunk, chunk), chunk)
        total = None
        for terms, source in ((kept, columns), (received, other_columns)):
            for first in (0, half):
                at_columns = slice(first, first + half)
                block = source[at_columns, :]
                part = slopes_of(rows[at, :], block, terms, step, chunk, at_columns)
                if source is columns:
                    slopes[at, at_columns] = part
                part = jnp.dot(part, block, preferred_element_type=jnp.float32)
                total = part if total is None else total + part
        gradient[at, :] = total.astype(gradient.dtype)

    steps_of(rows.shape[0] // chunk, body)


def columns_kernel(total_rows, chunk, master, history, columns, sent_0, sent_1, mine, beside, others, slopes_0, slopes_1, *outs):
    new_master, new_history, total = outs
    group_rows = mine.shape[0]
    total[...] = jnp.zeros_like(total)

    def body(step):
        first = pl.multiple_of(step * chunk, chunk)
        at = pl.ds(first, chunk)
        part = total[...]
        for place in range(2):
            rows = (mine, beside)[place][at, :]
            own = (slopes_0, slopes_1)[place][at, :]
            part += lax.dot_general(own, rows, (((0,), (0,)), ((), ())), preferred_element_type=jnp.float32)
            rows = others[pl.ds(place * group_rows + first, chunk), :]
            own = slopes_of(rows, columns[...], (sent_0, sent_1)[place], step, chunk)
            part += lax.dot_general(own, rows, (((0,), (0,)), ((), ())), preferred_element_type=jnp.float32)
        total[...] = part

    steps_of(group_rows // chunk, body)
    gradient = total[...] / total_rows
    updated = history[...] + gradient * gradient
    new_history[...] = updated
    new_master[...] = master[...] - step_size * gradient * lax.rsqrt(updated)


def place_kernel(*refs):
    pieces, out = refs[:4], refs[4]
    for place in range(4):
        for g in range(pieces[0].shape[0]):
            out[place_at(place, g)] = pieces[place][g]


def joined(held, other, upper):
    low, high = jnp.where(upper, other, held), jnp.where(upper, held, other)
    return jnp.stack([low, high], axis=1).reshape((2 * held.shape[0],) + held.shape[1:])


def per_device(
    counts, row_totals, column_totals, row_master, row_history, column_master, column_history
):
    size = lax.axis_size("col")
    me = lax.axis_index("col")
    total_rows, block_columns = counts.shape
    all_columns = block_columns * size
    own, width = row_master.shape
    group = size // 4
    group_rows = group * own
    chunk = 128
    terms_type = pltpu.VMEM((2, group, own, block_columns), jnp.float32)

    grid = (group // 2, 2, 2, 2, own)
    kept_0, kept_1, sent_0, sent_1, column_copy, row_copy, history, side = pl.pallas_call(
        prepare_kernel,
        out_shape=(terms_type,) * 4 + (pltpu.VMEM(column_master.shape, jnp.bfloat16), pltpu.VMEM(row_master.shape, jnp.float32), pltpu.VMEM(row_master.shape, jnp.bfloat16), pltpu.VMEM((8, width), jnp.float32)),
        in_specs=[HBM] * 6,
        out_specs=[VMEM] * 8,
        scratch_shapes=[
            pltpu.VMEM(grid + (block_columns,), jnp.int32),
            pltpu.VMEM((1, total_rows), jnp.int32),
            pltpu.VMEM((1, block_columns), jnp.int32),
            pltpu.VMEM(column_master.shape, jnp.float32),
            pltpu.VMEM(row_history.shape, jnp.float32),
            pltpu.VMEM(grid + (128,), jnp.float32),
            pltpu.SemaphoreType.DMA((6,)),
        ],
        compiler_params=PARAMS,
        cost_estimate=pl.CostEstimate(flops=8 * counts.size, bytes_accessed=4 * counts.size, transcendentals=2 * counts.size),
        name="prepare",
    )(
        far(counts.reshape(grid + (block_columns,))),
        far(row_totals.reshape(1, total_rows)),
        far(column_totals.reshape(1, block_columns)),
        far(column_master),
        far(row_master),
        far(row_history),
    )
    other_columns = hop(column_copy, CORE, size)
    received_0, received_1 = hop(sent_0, CORE, size), hop(sent_1, CORE, size)
    steps = [((bit, bit), side[k] > 0) for k, bit in enumerate(top_bits(size))]
    steps.append((SUM, side[len(steps)] > 0))
    first_hop = hop(row_master[None], steps[0][0], size)
    master, other = row_copy[None], first_hop
    for k, (bits, upper) in enumerate(steps):
        if k > 0:
            other = hop(master, bits, size)
        master = joined(master, other, upper).astype(jnp.bfloat16)
    mine = master.reshape(group_rows, width)
    beside = hop(mine, SPLIT, size)
    history, _ = lax.optimization_barrier((history[None], mine))
    for bits, upper in steps[:-1]:
        history = joined(history, hop(history, bits, size), upper)

    def gradient_of(kind, rows, kept, received, *after):
        return pl.pallas_call(
            functools.partial(rows_kernel, chunk),
            out_shape=(pltpu.VMEM((group_rows, width), kind), pltpu.VMEM((group_rows, block_columns), jnp.bfloat16)),
            in_specs=[VMEM] * 5 + [ANY] * len(after),
            out_specs=[VMEM] * 2,
            compiler_params=PARAMS,
            cost_estimate=pl.CostEstimate(flops=8 * group_rows * block_columns * width, bytes_accessed=0, transcendentals=4 * group_rows * block_columns),
            name="rows",
        )(*[near(v) for v in (rows, kept, received, column_copy, other_columns)], *after)

    part_late, slopes_1 = gradient_of(jnp.bfloat16, beside, kept_1, received_1)
    part_early, slopes_0 = gradient_of(jnp.float32, mine, kept_0, received_0, first_hop)
    own_rows, part_late = lax.optimization_barrier((jnp.concatenate([mine, beside]), part_late))
    others = hop(own_rows, CORE, size)
    others, history = lax.optimization_barrier((others, history))

    part = part_early + hop(part_late, SPLIT, size).astype(jnp.float32)
    struct = jax.ShapeDtypeStruct(column_master.shape, jnp.float32)
    new_columns, new_column_history = pl.pallas_call(
        functools.partial(columns_kernel, total_rows, chunk),
        out_shape=(struct, struct),
        in_specs=[VMEM] * 10,
        out_specs=[VMEM] * 2,
        scratch_shapes=[pltpu.VMEM(column_master.shape, jnp.float32)],
        compiler_params=PARAMS,
        cost_estimate=pl.CostEstimate(flops=2 * total_rows * block_columns * width, bytes_accessed=4 * column_master.size * 4, transcendentals=0),
        name="columns",
    )(*[near(v) for v in (column_master, column_history, column_copy, sent_0, sent_1, mine, beside, others, slopes_0, slopes_1)])

    last_history = hop(history, SUM, size)
    for bits, upper in steps:
        rounded = part.astype(jnp.bfloat16)
        part = rounded.astype(jnp.float32) + hop(rounded, bits, size).astype(jnp.float32)
    history = joined(history, last_history, steps[-1][1])

    def adagrad(master, history, gradient):
        updated = history + gradient * gradient
        return master - step_size * gradient * lax.rsqrt(updated), updated

    gradient = part.reshape(group, own, width) / all_columns
    own_gradient = lax.dynamic_index_in_dim(gradient, (me >> 3) * 2 + last_bit(me), 0, keepdims=False)
    new_rows, new_row_history = adagrad(row_master, row_history, own_gradient)
    copy = adagrad(master.astype(jnp.float32), history.astype(jnp.float32), gradient)[0].astype(jnp.bfloat16)
    beside = hop(copy, SPLIT, size)
    beside, new_columns = lax.optimization_barrier((beside, new_columns))
    grid_rows = pl.pallas_call(
        place_kernel,
        out_shape=jax.ShapeDtypeStruct(grid + (width,), jnp.bfloat16),
        in_specs=[VMEM] * 4,
        out_specs=VMEM,
        compiler_params=PARAMS,
        name="place",
    )(near(copy), near(beside), near(hop(copy, CORE, size)), near(hop(beside, CORE, size)))
    return (grid_rows.reshape(total_rows, width), new_rows, new_row_history, new_columns, new_column_history)


def solution(mesh):
    return jax.shard_map(
        per_device,
        mesh=mesh,
        in_specs=(
            P("parts", "col"),
            P("parts"),
            P(("parts", "col")),
            P(("parts", "col"), None),
            P(("parts", "col"), None),
            P(("parts", "col"), None),
            P(("parts", "col"), None),
        ),
        out_specs=(
            P("parts", None),
            P(("parts", "col"), None),
            P(("parts", "col"), None),
            P(("parts", "col"), None),
            P(("parts", "col"), None),
        ),
        check_vma=False,
    )
```

```python
import functools

import jax
import jax.numpy as jnp
from jax import lax
from jax.experimental import pallas as pl
from jax.experimental.pallas import tpu as pltpu
from jax.sharding import PartitionSpec as P

step_size = 2.0
VMEM = pl.BlockSpec(memory_space=pltpu.VMEM)
HBM = pl.BlockSpec(memory_space=pltpu.HBM)
ANY = pl.BlockSpec(memory_space=pl.ANY)
PARAMS = pltpu.CompilerParams(vmem_limit_bytes=20 * 1024 * 1024)


def parity(value):
    for shift in (4, 2, 1):
        value = value ^ (value >> shift)
    return value & 1


def top_bits(size):
    return [size >> k for k in range(1, size.bit_length() - 3)]


def last_bit(me):
    return ((me >> 2) ^ (parity(me) & ((me >> 1) ^ (me >> 2)))) & 1


def hop(value, bits, size):
    pairs = [(i, i ^ (bits[parity(i)] | 1)) for i in range(size)]
    return lax.ppermute(value, "col", pairs)


CORE, SPLIT, SUM = (1, 1), (2, 4), (4, 2)


def near(value):
    return pltpu.with_memory_space_constraint(value, pltpu.VMEM)


def far(value):
    return pltpu.with_memory_space_constraint(value, pltpu.HBM)


def place_at(place, g):
    me = lax.axis_index("col")
    odd = parity(me) ^ (place >> 1)
    one, two = (me >> 1) & 1, (me >> 2) & 1
    split, last, rest = (one + odd * (two - one)) ^ (place & 1), g & 1, g >> 1
    bit_one, bit_two = split + odd * (last - split), last + odd * (split - last)
    return rest, bit_two, bit_one, odd ^ bit_one ^ bit_two ^ parity(rest)


def steps_of(count, body):
    if count == 1:
        body(0)
    else:
        pl.loop(0, count)(body)


def prepare_kernel(counts, row_totals, column_totals, columns, rows, history, *refs):
    kept_0, kept_1, sent_0, sent_1, column_copy, row_copy, history_copy, upper, turned = refs[:9]
    near_counts, near_rows, near_columns, near_copy, near_history, row_terms, sems = refs[9:]
    groups = kept_0.shape[1]
    copies = [
        pltpu.make_async_copy(row_totals, near_rows, sems.at[0]),
        pltpu.make_async_copy(column_totals, near_columns, sems.at[1]),
        pltpu.make_async_copy(counts, near_counts, sems.at[2]),
        pltpu.make_async_copy(columns, near_copy, sems.at[3]),
        pltpu.make_async_copy(rows, row_copy, sems.at[4]),
        pltpu.make_async_copy(history, near_history, sems.at[5]),
    ]
    for copy in copies:
        copy.start()
    me = lax.axis_index("col")
    changed = [(me // bit) & 1 for bit in top_bits(8 * counts.shape[0])] + [last_bit(me)]
    step = lax.broadcasted_iota(jnp.int32, upper.shape, 0)
    upper[...] = sum(jnp.where(step == k, bit, 0) for k, bit in enumerate(changed)).astype(jnp.float32)
    copies[0].wait()
    row_floats = near_rows[...].astype(jnp.float32)
    terms = jnp.log(jnp.sum(row_floats, axis=1, keepdims=True)) - jnp.log(row_floats)
    row_terms[...] = jnp.broadcast_to(terms, (128, terms.shape[1])).T.reshape(row_terms.shape)
    copies[1].wait()
    column_term = jnp.log(near_columns[...].astype(jnp.float32))
    copies[2].wait()
    for place in range(4):

        def body(g, place=place):
            at = place_at(place, g)
            amounts = near_counts[at].astype(jnp.float32)
            term = row_terms[at]
            term = jnp.concatenate([term] * (amounts.shape[1] // 128), axis=1)
            target = (kept_0, kept_1, sent_0, sent_1)[place]
            target[0, g] = jnp.log(jnp.maximum(amounts, 1.0)) + (term - column_term)
            target[1, g] = jnp.where(amounts > 0, 0.1 + 0.25 * jnp.sqrt(amounts), 0.0)

        if groups <= 4:
            for g in range(groups):
                body(g)
        else:
            pl.loop(0, groups)(body)
    copies[3].wait()
    column_copy[...] = near_copy[...].astype(jnp.bfloat16)
    turned[...] = near_copy[...].T.astype(jnp.bfloat16)
    copies[4].wait()
    copies[5].wait()
    history_copy[...] = near_history[...].astype(jnp.bfloat16)


def slopes_of(rows, columns, terms, step, chunk, at_columns=slice(None)):
    group = chunk // terms.shape[2]
    at = pl.ds(step * group, group)
    scores = jnp.dot(rows, columns, preferred_element_type=jnp.float32)
    gap = scores - terms[0, at, :, at_columns].reshape(scores.shape)
    confidence = terms[1, at, :, at_columns].reshape(scores.shape)
    return jnp.where(confidence > 0, confidence * gap, jax.nn.sigmoid(gap)).astype(jnp.bfloat16)


def rows_kernel(chunk, rows, kept, received, columns, other_columns, turned, *refs):
    gradient, slopes = refs[-2:]
    half = columns.shape[0] // 2

    def body(step):
        at = pl.ds(pl.multiple_of(step * chunk, chunk), chunk)
        total = None
        for terms, source, across in ((kept, columns, turned), (received, other_columns, other_columns[...].T)):
            for first in (0, half):
                at_columns = slice(first, first + half)
                part = slopes_of(rows[at, :], across[:, at_columns], terms, step, chunk, at_columns)
                if source is columns:
                    slopes[at, at_columns] = part
                part = jnp.dot(part, source[at_columns, :], preferred_element_type=jnp.float32)
                total = part if total is None else total + part
        gradient[at, :] = total.astype(gradient.dtype)

    steps_of(rows.shape[0] // chunk, body)


def columns_kernel(total_rows, chunk, master, history, turned, sent_0, sent_1, mine, beside, others, slopes_0, slopes_1, *refs):
    new_master, new_history, far_slopes, near_master, near_history, sems = refs
    group_rows, half, block = mine.shape[0], turned.shape[1] // 2, 128

    def body(step):
        first = pl.multiple_of(step * chunk, chunk)
        for place in range(2):
            at = pl.ds(place * group_rows + first, chunk)
            for start in (0, half):
                at_columns = slice(start, start + half)
                far_slopes[at, at_columns] = slopes_of(
                    others[at, :], turned[:, at_columns], (sent_0, sent_1)[place], step, chunk, at_columns
                )

    steps_of(group_rows // chunk, body)
    copies = []
    for k in range(turned.shape[1] // block):
        at = slice(k * block, (k + 1) * block)
        total = None
        for rows, slopes in ((mine, slopes_0), (beside, slopes_1), (others, far_slopes)):
            part = lax.dot_general(slopes[:, at], rows[...], (((0,), (0,)), ((), ())), preferred_element_type=jnp.float32)
            total = part if total is None else total + part
        gradient = total / total_rows
        updated = history[at, :] + gradient * gradient
        near_history[at, :] = updated
        near_master[at, :] = master[at, :] - step_size * gradient * lax.rsqrt(updated)
        copies.append(pltpu.make_async_copy(near_history.at[at, :], new_history.at[at, :], sems.at[2 * k]))
        copies.append(pltpu.make_async_copy(near_master.at[at, :], new_master.at[at, :], sems.at[2 * k + 1]))
        copies[-2].start()
        copies[-1].start()
    for copy in copies:
        copy.wait()


def place_kernel(*refs):
    pieces, out = refs[:4], refs[4]
    for place in range(4):
        for g in range(pieces[0].shape[0]):
            out[place_at(place, g)] = pieces[place][g]


def joined(held, other, upper):
    low, high = jnp.where(upper, other, held), jnp.where(upper, held, other)
    return jnp.stack([low, high], axis=1).reshape((2 * held.shape[0],) + held.shape[1:])


def per_device(
    counts, row_totals, column_totals, row_master, row_history, column_master, column_history
):
    size = lax.axis_size("col")
    me = lax.axis_index("col")
    total_rows, block_columns = counts.shape
    all_columns = block_columns * size
    own, width = row_master.shape
    group = size // 4
    group_rows = group * own
    chunk = 128
    terms_type = pltpu.VMEM((2, group, own, block_columns), jnp.float32)

    grid = (group // 2, 2, 2, 2, own)
    kept_0, kept_1, sent_0, sent_1, column_copy, row_copy, history, side, turned = pl.pallas_call(
        prepare_kernel,
        out_shape=(terms_type,) * 4 + (pltpu.VMEM(column_master.shape, jnp.bfloat16), pltpu.VMEM(row_master.shape, jnp.float32), pltpu.VMEM(row_master.shape, jnp.bfloat16), pltpu.VMEM((8, width), jnp.float32), pltpu.VMEM((width, block_columns), jnp.bfloat16)),
        in_specs=[HBM] * 6,
        out_specs=[VMEM] * 9,
        scratch_shapes=[
            pltpu.VMEM(grid + (block_columns,), jnp.int32),
            pltpu.VMEM((1, total_rows), jnp.int32),
            pltpu.VMEM((1, block_columns), jnp.int32),
            pltpu.VMEM(column_master.shape, jnp.float32),
            pltpu.VMEM(row_history.shape, jnp.float32),
            pltpu.VMEM(grid + (128,), jnp.float32),
            pltpu.SemaphoreType.DMA((6,)),
        ],
        compiler_params=PARAMS,
        cost_estimate=pl.CostEstimate(flops=8 * counts.size, bytes_accessed=4 * counts.size, transcendentals=2 * counts.size),
        name="prepare",
    )(
        far(counts.reshape(grid + (block_columns,))),
        far(row_totals.reshape(1, total_rows)),
        far(column_totals.reshape(1, block_columns)),
        far(column_master),
        far(row_master),
        far(row_history),
    )
    other_columns = hop(column_copy, CORE, size)
    received_0, received_1 = hop(sent_0, CORE, size), hop(sent_1, CORE, size)
    steps = [((bit, bit), side[k] > 0) for k, bit in enumerate(top_bits(size))]
    steps.append((SUM, side[len(steps)] > 0))
    first_hop = hop(row_master[None], steps[0][0], size)
    master, other = row_copy[None], first_hop
    for k, (bits, upper) in enumerate(steps):
        if k > 0:
            other = hop(master, bits, size)
        master = joined(master, other, upper).astype(jnp.bfloat16)
    mine = master.reshape(group_rows, width)
    beside = hop(mine, SPLIT, size)
    history, _ = lax.optimization_barrier((history[None], mine))
    for bits, upper in steps[:-1]:
        history = joined(history, hop(history, bits, size), upper)

    def gradient_of(kind, rows, kept, received, *after):
        return pl.pallas_call(
            functools.partial(rows_kernel, chunk),
            out_shape=(pltpu.VMEM((group_rows, width), kind), pltpu.VMEM((group_rows, block_columns), jnp.bfloat16)),
            in_specs=[VMEM] * 6 + [ANY] * len(after),
            out_specs=[VMEM] * 2,
            compiler_params=PARAMS,
            cost_estimate=pl.CostEstimate(flops=8 * group_rows * block_columns * width, bytes_accessed=0, transcendentals=4 * group_rows * block_columns),
            name="rows",
        )(*[near(v) for v in (rows, kept, received, column_copy, other_columns, turned)], *after)

    part_late, slopes_1 = gradient_of(jnp.bfloat16, beside, kept_1, received_1)
    part_early, slopes_0 = gradient_of(jnp.float32, mine, kept_0, received_0, first_hop)
    own_rows, part_late = lax.optimization_barrier((jnp.concatenate([mine, beside]), part_late))
    others = hop(own_rows, CORE, size)
    others, history = lax.optimization_barrier((others, history))

    part = part_early + hop(part_late, SPLIT, size).astype(jnp.float32)
    struct = jax.ShapeDtypeStruct(column_master.shape, jnp.float32)
    new_columns, new_column_history = pl.pallas_call(
        functools.partial(columns_kernel, total_rows, chunk),
        out_shape=(struct, struct),
        in_specs=[VMEM] * 10,
        out_specs=[HBM] * 2,
        scratch_shapes=[
            pltpu.VMEM((2 * group_rows, block_columns), jnp.bfloat16),
            pltpu.VMEM(column_master.shape, jnp.float32),
            pltpu.VMEM(column_master.shape, jnp.float32),
            pltpu.SemaphoreType.DMA((2 * (block_columns // 128),)),
        ],
        compiler_params=PARAMS,
        cost_estimate=pl.CostEstimate(flops=2 * total_rows * block_columns * width, bytes_accessed=4 * column_master.size * 4, transcendentals=0),
        name="columns",
    )(*[near(v) for v in (column_master, column_history, turned, sent_0, sent_1, mine, beside, others, slopes_0, slopes_1)])

    last_history = hop(history, SUM, size)
    for bits, upper in steps:
        rounded = part.astype(jnp.bfloat16)
        part = rounded.astype(jnp.float32) + hop(rounded, bits, size).astype(jnp.float32)
    history = joined(history, last_history, steps[-1][1])

    def adagrad(master, history, gradient):
        updated = history + gradient * gradient
        return master - step_size * gradient * lax.rsqrt(updated), updated

    gradient = part.reshape(group, own, width) / all_columns
    own_gradient = lax.dynamic_index_in_dim(gradient, (me >> 3) * 2 + last_bit(me), 0, keepdims=False)
    new_rows, new_row_history = adagrad(row_master, row_history, own_gradient)
    copy = adagrad(master.astype(jnp.float32), history.astype(jnp.float32), gradient)[0].astype(jnp.bfloat16)
    beside = hop(copy, SPLIT, size)
    beside, new_columns = lax.optimization_barrier((beside, new_columns))
    grid_rows = pl.pallas_call(
        place_kernel,
        out_shape=jax.ShapeDtypeStruct(grid + (width,), jnp.bfloat16),
        in_specs=[VMEM] * 4,
        out_specs=VMEM,
        compiler_params=PARAMS,
        name="place",
    )(near(copy), near(beside), near(hop(copy, CORE, size)), near(hop(beside, CORE, size)))
    return (grid_rows.reshape(total_rows, width), new_rows, new_row_history, new_columns, new_column_history)


def solution(mesh):
    return jax.shard_map(
        per_device,
        mesh=mesh,
        in_specs=(
            P("parts", "col"),
            P("parts"),
            P(("parts", "col")),
            P(("parts", "col"), None),
            P(("parts", "col"), None),
            P(("parts", "col"), None),
            P(("parts", "col"), None),
        ),
        out_specs=(
            P("parts", None),
            P(("parts", "col"), None),
            P(("parts", "col"), None),
            P(("parts", "col"), None),
            P(("parts", "col"), None),
        ),
        check_vma=False,
    )
```

```python
import functools

import jax
import jax.numpy as jnp
from jax import lax
from jax.experimental import pallas as pl
from jax.experimental.pallas import tpu as pltpu
from jax.sharding import PartitionSpec as P

step_size = 2.0
VMEM = pl.BlockSpec(memory_space=pltpu.VMEM)
HBM = pl.BlockSpec(memory_space=pltpu.HBM)
ANY = pl.BlockSpec(memory_space=pl.ANY)
PARAMS = pltpu.CompilerParams(vmem_limit_bytes=20 * 1024 * 1024)


def parity(value):
    for shift in (4, 2, 1):
        value = value ^ (value >> shift)
    return value & 1


def top_bits(size):
    return [size >> k for k in range(1, size.bit_length() - 3)]


def last_bit(me):
    return ((me >> 2) ^ (parity(me) & ((me >> 1) ^ (me >> 2)))) & 1


def hop(value, bits, size):
    pairs = [(i, i ^ (bits[parity(i)] | 1)) for i in range(size)]
    return lax.ppermute(value, "col", pairs)


CORE, SPLIT, SUM = (1, 1), (2, 4), (4, 2)


def near(value):
    return pltpu.with_memory_space_constraint(value, pltpu.VMEM)


def far(value):
    return pltpu.with_memory_space_constraint(value, pltpu.HBM)


def place_at(place, g, groups):
    me = lax.axis_index("col")
    odd = parity(me) ^ (place >> 1)
    one, two = (me >> 1) & 1, (me >> 2) & 1
    split, last, rest = (one + odd * (two - one)) ^ (place & 1), g // (groups // 2), g % (groups // 2)
    bit_one, bit_two = split + odd * (last - split), last + odd * (split - last)
    return rest, bit_two, bit_one, odd ^ bit_one ^ bit_two ^ parity(rest)


def steps_of(count, body):
    if count == 1:
        body(0)
    else:
        pl.loop(0, count)(body)


def prepare_kernel(counts, row_totals, column_totals, columns, rows, history, *refs):
    kept_0, kept_1, sent_0, sent_1, column_copy, row_copy, history_copy, upper, turned = refs[:9]
    near_counts, near_rows, near_columns, near_copy, near_history, row_terms, sems = refs[9:]
    groups = kept_0.shape[1]
    copies = [
        pltpu.make_async_copy(row_totals, near_rows, sems.at[0]),
        pltpu.make_async_copy(column_totals, near_columns, sems.at[1]),
        pltpu.make_async_copy(counts, near_counts, sems.at[2]),
        pltpu.make_async_copy(columns, near_copy, sems.at[3]),
        pltpu.make_async_copy(rows, row_copy, sems.at[4]),
        pltpu.make_async_copy(history, near_history, sems.at[5]),
    ]
    for copy in copies:
        copy.start()
    me = lax.axis_index("col")
    changed = [(me // bit) & 1 for bit in top_bits(8 * counts.shape[0])] + [last_bit(me)]
    step = lax.broadcasted_iota(jnp.int32, upper.shape, 0)
    upper[...] = sum(jnp.where(step == k, bit, 0) for k, bit in enumerate(changed)).astype(jnp.float32)
    copies[0].wait()
    row_floats = near_rows[...].astype(jnp.float32)
    terms = jnp.log(jnp.sum(row_floats, axis=1, keepdims=True)) - jnp.log(row_floats)
    row_terms[...] = jnp.broadcast_to(terms, (128, terms.shape[1])).T.reshape(row_terms.shape)
    copies[1].wait()
    column_term = jnp.log(near_columns[...].astype(jnp.float32))
    copies[2].wait()
    for place in range(4):

        def body(g, place=place):
            at = place_at(place, g, groups)
            amounts = near_counts[at].astype(jnp.float32)
            term = row_terms[at]
            term = jnp.concatenate([term] * (amounts.shape[1] // 128), axis=1)
            target = (kept_0, kept_1, sent_0, sent_1)[place]
            target[0, g] = jnp.log(jnp.maximum(amounts, 1.0)) + (term - column_term)
            target[1, g] = jnp.where(amounts > 0, 0.1 + 0.25 * jnp.sqrt(amounts), 0.0)

        if groups <= 4:
            for g in range(groups):
                body(g)
        else:
            pl.loop(0, groups)(body)
    copies[3].wait()
    column_copy[...] = near_copy[...].astype(jnp.bfloat16)
    turned[...] = near_copy[...].T.astype(jnp.bfloat16)
    copies[4].wait()
    copies[5].wait()
    history_copy[...] = near_history[...].astype(jnp.bfloat16)


def slopes_of(rows, columns, terms, step, chunk, at_columns=slice(None)):
    group = chunk // terms.shape[2]
    at = pl.ds(step * group, group)
    scores = jnp.dot(rows, columns, preferred_element_type=jnp.float32)
    gap = scores - terms[0, at, :, at_columns].reshape(scores.shape)
    confidence = terms[1, at, :, at_columns].reshape(scores.shape)
    return jnp.where(confidence > 0, confidence * gap, jax.nn.sigmoid(gap)).astype(jnp.bfloat16)


def rows_kernel(chunk, rows, kept, received, columns, other_columns, turned, *refs):
    gradient, slopes = refs[-2:]
    half = columns.shape[0] // 2

    def body(step):
        at = pl.ds(pl.multiple_of(step * chunk, chunk), chunk)
        total = None
        for terms, source, across in ((kept, columns, turned), (received, other_columns, other_columns[...].T)):
            for first in (0, half):
                at_columns = slice(first, first + half)
                part = slopes_of(rows[at, :], across[:, at_columns], terms, step, chunk, at_columns)
                if source is columns:
                    slopes[at, at_columns] = part
                part = jnp.dot(part, source[at_columns, :], preferred_element_type=jnp.float32)
                total = part if total is None else total + part
        gradient[at, :] = total.astype(gradient.dtype)

    steps_of(rows.shape[0] // chunk, body)


def columns_kernel(total_rows, chunk, master, history, turned, sent_0, sent_1, mine, beside, others, slopes_0, slopes_1, *refs):
    new_master, new_history, far_slopes, near_master, near_history, sems = refs
    group_rows, half, block = mine.shape[0], turned.shape[1] // 2, 128

    def body(step):
        first = pl.multiple_of(step * chunk, chunk)
        for place in range(2):
            at = pl.ds(place * group_rows + first, chunk)
            for start in (0, half):
                at_columns = slice(start, start + half)
                far_slopes[at, at_columns] = slopes_of(
                    others[at, :], turned[:, at_columns], (sent_0, sent_1)[place], step, chunk, at_columns
                )

    steps_of(group_rows // chunk, body)
    copies = []
    for k in range(turned.shape[1] // block):
        at = slice(k * block, (k + 1) * block)
        total = None
        for rows, slopes in ((mine, slopes_0), (beside, slopes_1), (others, far_slopes)):
            part = lax.dot_general(slopes[:, at], rows[...], (((0,), (0,)), ((), ())), preferred_element_type=jnp.float32)
            total = part if total is None else total + part
        gradient = total / total_rows
        updated = history[at, :] + gradient * gradient
        near_history[at, :] = updated
        near_master[at, :] = master[at, :] - step_size * gradient * lax.rsqrt(updated)
        copies.append(pltpu.make_async_copy(near_history.at[at, :], new_history.at[at, :], sems.at[2 * k]))
        copies.append(pltpu.make_async_copy(near_master.at[at, :], new_master.at[at, :], sems.at[2 * k + 1]))
        copies[-2].start()
        copies[-1].start()
    for copy in copies:
        copy.wait()


def place_kernel(*refs):
    pieces, out = refs[:4], refs[4]
    for place in range(4):
        for g in range(pieces[0].shape[0]):
            out[place_at(place, g, pieces[0].shape[0])] = pieces[place][g]


def joined(held, other, upper):
    low, high = jnp.where(upper, other, held), jnp.where(upper, held, other)
    return jnp.stack([low, high], axis=1).reshape((2 * held.shape[0],) + held.shape[1:])


def per_device(
    counts, row_totals, column_totals, row_master, row_history, column_master, column_history
):
    size = lax.axis_size("col")
    me = lax.axis_index("col")
    total_rows, block_columns = counts.shape
    all_columns = block_columns * size
    own, width = row_master.shape
    group = size // 4
    group_rows = group * own
    chunk = 128
    terms_type = pltpu.VMEM((2, group, own, block_columns), jnp.float32)

    grid = (group // 2, 2, 2, 2, own)
    kept_0, kept_1, sent_0, sent_1, column_copy, row_copy, history, side, turned = pl.pallas_call(
        prepare_kernel,
        out_shape=(terms_type,) * 4 + (pltpu.VMEM(column_master.shape, jnp.bfloat16), pltpu.VMEM(row_master.shape, jnp.float32), pltpu.VMEM(row_master.shape, jnp.bfloat16), pltpu.VMEM((8, width), jnp.float32), pltpu.VMEM((width, block_columns), jnp.bfloat16)),
        in_specs=[HBM] * 6,
        out_specs=[VMEM] * 9,
        scratch_shapes=[
            pltpu.VMEM(grid + (block_columns,), jnp.int32),
            pltpu.VMEM((1, total_rows), jnp.int32),
            pltpu.VMEM((1, block_columns), jnp.int32),
            pltpu.VMEM(column_master.shape, jnp.float32),
            pltpu.VMEM(row_history.shape, jnp.float32),
            pltpu.VMEM(grid + (128,), jnp.float32),
            pltpu.SemaphoreType.DMA((6,)),
        ],
        compiler_params=PARAMS,
        cost_estimate=pl.CostEstimate(flops=8 * counts.size, bytes_accessed=4 * counts.size, transcendentals=2 * counts.size),
        name="prepare",
    )(
        far(counts.reshape(grid + (block_columns,))),
        far(row_totals.reshape(1, total_rows)),
        far(column_totals.reshape(1, block_columns)),
        far(column_master),
        far(row_master),
        far(row_history),
    )
    other_columns = hop(column_copy, CORE, size)
    received_0, received_1 = hop(sent_0, CORE, size), hop(sent_1, CORE, size)
    steps = [((bit, bit), side[k] > 0) for k, bit in enumerate(top_bits(size))]
    steps.append((SUM, side[len(steps)] > 0))
    gathers = steps[-1:] + steps[:-1]
    first_hop = hop(row_master[None], gathers[0][0], size)
    master, other = row_copy[None], first_hop
    for k, (bits, upper) in enumerate(gathers):
        if k > 0:
            other = hop(master, bits, size)
        master = joined(master, other, upper).astype(jnp.bfloat16)
    mine = master.reshape(group_rows, width)
    beside = hop(mine, SPLIT, size)
    history, _ = lax.optimization_barrier((history[None], mine))
    for bits, upper in gathers[:-1]:
        history = joined(history, hop(history, bits, size), upper)

    def gradient_of(kind, rows, kept, received, *after):
        return pl.pallas_call(
            functools.partial(rows_kernel, chunk),
            out_shape=(pltpu.VMEM((group_rows, width), kind), pltpu.VMEM((group_rows, block_columns), jnp.bfloat16)),
            in_specs=[VMEM] * 6 + [ANY] * len(after),
            out_specs=[VMEM] * 2,
            compiler_params=PARAMS,
            cost_estimate=pl.CostEstimate(flops=8 * group_rows * block_columns * width, bytes_accessed=0, transcendentals=4 * group_rows * block_columns),
            name="rows",
        )(*[near(v) for v in (rows, kept, received, column_copy, other_columns, turned)], *after)

    part_late, slopes_1 = gradient_of(jnp.bfloat16, beside, kept_1, received_1)
    part_early, slopes_0 = gradient_of(jnp.float32, mine, kept_0, received_0, first_hop)
    own_rows, part_late = lax.optimization_barrier((jnp.concatenate([mine, beside]), part_late))
    others = hop(own_rows, CORE, size)
    others, history = lax.optimization_barrier((others, history))

    part = part_early + hop(part_late, SPLIT, size).astype(jnp.float32)
    struct = jax.ShapeDtypeStruct(column_master.shape, jnp.float32)
    new_columns, new_column_history = pl.pallas_call(
        functools.partial(columns_kernel, total_rows, chunk),
        out_shape=(struct, struct),
        in_specs=[VMEM] * 10,
        out_specs=[HBM] * 2,
        scratch_shapes=[
            pltpu.VMEM((2 * group_rows, block_columns), jnp.bfloat16),
            pltpu.VMEM(column_master.shape, jnp.float32),
            pltpu.VMEM(column_master.shape, jnp.float32),
            pltpu.SemaphoreType.DMA((2 * (block_columns // 128),)),
        ],
        compiler_params=PARAMS,
        cost_estimate=pl.CostEstimate(flops=2 * total_rows * block_columns * width, bytes_accessed=4 * column_master.size * 4, transcendentals=0),
        name="columns",
    )(*[near(v) for v in (column_master, column_history, turned, sent_0, sent_1, mine, beside, others, slopes_0, slopes_1)])

    last_history = hop(history, gathers[-1][0], size)
    for bits, upper in steps:
        rounded = part.astype(jnp.bfloat16)
        part = rounded.astype(jnp.float32) + hop(rounded, bits, size).astype(jnp.float32)
    history = joined(history, last_history, gathers[-1][1])

    def adagrad(master, history, gradient):
        updated = history + gradient * gradient
        return master - step_size * gradient * lax.rsqrt(updated), updated

    gradient = part.reshape(group, own, width) / all_columns
    own_gradient = lax.dynamic_index_in_dim(gradient, last_bit(me) * (group // 2) + (me >> 3), 0, keepdims=False)
    new_rows, new_row_history = adagrad(row_master, row_history, own_gradient)
    copy = adagrad(master.astype(jnp.float32), history.astype(jnp.float32), gradient)[0].astype(jnp.bfloat16)
    beside = hop(copy, SPLIT, size)
    beside, new_columns = lax.optimization_barrier((beside, new_columns))
    grid_rows = pl.pallas_call(
        place_kernel,
        out_shape=jax.ShapeDtypeStruct(grid + (width,), jnp.bfloat16),
        in_specs=[VMEM] * 4,
        out_specs=VMEM,
        compiler_params=PARAMS,
        name="place",
    )(near(copy), near(beside), near(hop(copy, CORE, size)), near(hop(beside, CORE, size)))
    return (grid_rows.reshape(total_rows, width), new_rows, new_row_history, new_columns, new_column_history)


def solution(mesh):
    return jax.shard_map(
        per_device,
        mesh=mesh,
        in_specs=(
            P("parts", "col"),
            P("parts"),
            P(("parts", "col")),
            P(("parts", "col"), None),
            P(("parts", "col"), None),
            P(("parts", "col"), None),
            P(("parts", "col"), None),
        ),
        out_specs=(
            P("parts", None),
            P(("parts", "col"), None),
            P(("parts", "col"), None),
            P(("parts", "col"), None),
            P(("parts", "col"), None),
        ),
        check_vma=False,
    )
```

```python
import functools

import jax
import jax.numpy as jnp
from jax import lax
from jax.experimental import pallas as pl
from jax.experimental.pallas import tpu as pltpu
from jax.sharding import PartitionSpec as P

step_size = 2.0
VMEM = pl.BlockSpec(memory_space=pltpu.VMEM)
HBM = pl.BlockSpec(memory_space=pltpu.HBM)
ANY = pl.BlockSpec(memory_space=pl.ANY)
PARAMS = pltpu.CompilerParams(vmem_limit_bytes=20 * 1024 * 1024)


def parity(value):
    for shift in (4, 2, 1):
        value = value ^ (value >> shift)
    return value & 1


def top_bits(size):
    return [size >> k for k in range(1, size.bit_length() - 3)]


def last_bit(me):
    return ((me >> 2) ^ (parity(me) & ((me >> 1) ^ (me >> 2)))) & 1


def hop(value, bits, size):
    pairs = [(i, i ^ (bits[parity(i)] | 1)) for i in range(size)]
    return lax.ppermute(value, "col", pairs)


CORE, SPLIT, SUM = (1, 1), (2, 4), (4, 2)


def near(value):
    return pltpu.with_memory_space_constraint(value, pltpu.VMEM)


def far(value):
    return pltpu.with_memory_space_constraint(value, pltpu.HBM)


def place_at(place, g, groups):
    me = lax.axis_index("col")
    odd = parity(me) ^ (place >> 1)
    one, two = (me >> 1) & 1, (me >> 2) & 1
    split, last, rest = (one + odd * (two - one)) ^ (place & 1), g // (groups // 2), g % (groups // 2)
    bit_one, bit_two = split + odd * (last - split), last + odd * (split - last)
    return rest, bit_two, bit_one, odd ^ bit_one ^ bit_two ^ parity(rest)


def steps_of(count, body):
    if count == 1:
        body(0)
    else:
        pl.loop(0, count)(body)


def prepare_kernel(counts, row_totals, column_totals, columns, rows, history, *refs):
    kept_0, kept_1, sent_0, sent_1, column_copy, row_copy, history_copy, upper, turned = refs[:9]
    near_counts, near_rows, near_columns, near_copy, near_history, row_terms, sems = refs[9:]
    groups = kept_0.shape[1]
    copies = [
        pltpu.make_async_copy(row_totals, near_rows, sems.at[0]),
        pltpu.make_async_copy(column_totals, near_columns, sems.at[1]),
        pltpu.make_async_copy(counts, near_counts, sems.at[2]),
        pltpu.make_async_copy(columns, near_copy, sems.at[3]),
        pltpu.make_async_copy(rows, row_copy, sems.at[4]),
        pltpu.make_async_copy(history, near_history, sems.at[5]),
    ]
    for copy in copies:
        copy.start()
    me = lax.axis_index("col")
    changed = [(me // bit) & 1 for bit in top_bits(8 * counts.shape[0])] + [last_bit(me)]
    step = lax.broadcasted_iota(jnp.int32, upper.shape, 0)
    upper[...] = sum(jnp.where(step == k, bit, 0) for k, bit in enumerate(changed)).astype(jnp.float32)
    copies[0].wait()
    row_floats = near_rows[...].astype(jnp.float32)
    terms = jnp.log(jnp.sum(row_floats, axis=1, keepdims=True)) - jnp.log(row_floats)
    row_terms[...] = jnp.broadcast_to(terms, (128, terms.shape[1])).T.reshape(row_terms.shape)
    copies[1].wait()
    column_term = jnp.log(near_columns[...].astype(jnp.float32))
    copies[2].wait()
    for place in range(4):

        def body(g, place=place):
            at = place_at(place, g, groups)
            amounts = near_counts[at].astype(jnp.float32)
            term = row_terms[at]
            term = jnp.concatenate([term] * (amounts.shape[1] // 128), axis=1)
            target = (kept_0, kept_1, sent_0, sent_1)[place]
            target[0, g] = jnp.log(jnp.maximum(amounts, 1.0)) + (term - column_term)
            target[1, g] = jnp.where(amounts > 0, 0.1 + 0.25 * jnp.sqrt(amounts), 0.0)

        if groups <= 4:
            for g in range(groups):
                body(g)
        else:
            pl.loop(0, groups)(body)
    copies[3].wait()
    column_copy[...] = near_copy[...].astype(jnp.bfloat16)
    turned[...] = near_copy[...].T.astype(jnp.bfloat16)
    copies[4].wait()
    copies[5].wait()
    history_copy[...] = near_history[...].astype(jnp.bfloat16)


def slopes_of(rows, columns, terms, step, chunk, at_columns=slice(None)):
    group = chunk // terms.shape[2]
    at = pl.ds(step * group, group)
    scores = jnp.dot(rows, columns, preferred_element_type=jnp.float32)
    gap = scores - terms[0, at, :, at_columns].reshape(scores.shape)
    confidence = terms[1, at, :, at_columns].reshape(scores.shape)
    return jnp.where(confidence > 0, confidence * gap, jax.nn.sigmoid(gap)).astype(jnp.bfloat16)


def rows_kernel(chunk, rows, kept, received, columns, other_columns, turned, *refs):
    gradient, slopes = refs[-2:]
    half = columns.shape[0] // 2

    def body(step):
        at = pl.ds(pl.multiple_of(step * chunk, chunk), chunk)
        total = None
        for terms, source, across in ((kept, columns, turned), (received, other_columns, other_columns[...].T)):
            for first in (0, half):
                at_columns = slice(first, first + half)
                part = slopes_of(rows[at, :], across[:, at_columns], terms, step, chunk, at_columns)
                if source is columns:
                    slopes[at, at_columns] = part
                part = jnp.dot(part, source[at_columns, :], preferred_element_type=jnp.float32)
                total = part if total is None else total + part
        gradient[at, :] = total.astype(gradient.dtype)

    steps_of(rows.shape[0] // chunk, body)


def columns_kernel(total_rows, chunk, master, history, turned, sent_0, sent_1, mine, beside, others, slopes_0, slopes_1, *refs):
    new_master, new_history, far_slopes, near_master, near_history, sems = refs
    group_rows, half, block = mine.shape[0], turned.shape[1] // 2, 128

    def body(step):
        first = pl.multiple_of(step * chunk, chunk)
        for place in range(2):
            at = pl.ds(place * group_rows + first, chunk)
            for start in (0, half):
                at_columns = slice(start, start + half)
                far_slopes[at, at_columns] = slopes_of(
                    others[at, :], turned[:, at_columns], (sent_0, sent_1)[place], step, chunk, at_columns
                )

    steps_of(group_rows // chunk, body)
    copies = []
    for k in range(turned.shape[1] // block):
        at = slice(k * block, (k + 1) * block)
        total = None
        for rows, slopes in ((mine, slopes_0), (beside, slopes_1), (others, far_slopes)):
            part = lax.dot_general(slopes[:, at], rows[...], (((0,), (0,)), ((), ())), preferred_element_type=jnp.float32)
            total = part if total is None else total + part
        gradient = total / total_rows
        updated = history[at, :] + gradient * gradient
        near_history[at, :] = updated
        near_master[at, :] = master[at, :] - step_size * gradient * lax.rsqrt(updated)
        copies.append(pltpu.make_async_copy(near_history.at[at, :], new_history.at[at, :], sems.at[2 * k]))
        copies.append(pltpu.make_async_copy(near_master.at[at, :], new_master.at[at, :], sems.at[2 * k + 1]))
        copies[-2].start()
        copies[-1].start()
    for copy in copies:
        copy.wait()


def place_kernel(*refs):
    pieces, out = refs[:4], refs[4]
    for place in range(4):
        for g in range(pieces[0].shape[0]):
            out[place_at(place, g, pieces[0].shape[0])] = pieces[place][g]


def joined(held, other, upper):
    low, high = jnp.where(upper, other, held), jnp.where(upper, held, other)
    return jnp.stack([low, high], axis=1).reshape((2 * held.shape[0],) + held.shape[1:])


def per_device(
    counts, row_totals, column_totals, row_master, row_history, column_master, column_history
):
    size = lax.axis_size("col")
    me = lax.axis_index("col")
    total_rows, block_columns = counts.shape
    all_columns = block_columns * size
    own, width = row_master.shape
    group = size // 4
    group_rows = group * own
    chunk = 128
    terms_type = pltpu.VMEM((2, group, own, block_columns), jnp.float32)

    grid = (group // 2, 2, 2, 2, own)
    kept_0, kept_1, sent_0, sent_1, column_copy, row_copy, history, side, turned = pl.pallas_call(
        prepare_kernel,
        out_shape=(terms_type,) * 4 + (pltpu.VMEM(column_master.shape, jnp.bfloat16), pltpu.VMEM(row_master.shape, jnp.float32), pltpu.VMEM(row_master.shape, jnp.bfloat16), pltpu.VMEM((8, width), jnp.float32), pltpu.VMEM((width, block_columns), jnp.bfloat16)),
        in_specs=[HBM] * 6,
        out_specs=[VMEM] * 9,
        scratch_shapes=[
            pltpu.VMEM(grid + (block_columns,), jnp.int32),
            pltpu.VMEM((1, total_rows), jnp.int32),
            pltpu.VMEM((1, block_columns), jnp.int32),
            pltpu.VMEM(column_master.shape, jnp.float32),
            pltpu.VMEM(row_history.shape, jnp.float32),
            pltpu.VMEM(grid + (128,), jnp.float32),
            pltpu.SemaphoreType.DMA((6,)),
        ],
        compiler_params=PARAMS,
        cost_estimate=pl.CostEstimate(flops=8 * counts.size, bytes_accessed=4 * counts.size, transcendentals=2 * counts.size),
        name="prepare",
    )(
        far(counts.reshape(grid + (block_columns,))),
        far(row_totals.reshape(1, total_rows)),
        far(column_totals.reshape(1, block_columns)),
        far(column_master),
        far(row_master),
        far(row_history),
    )
    other_columns = hop(column_copy, CORE, size)
    received_0, received_1 = hop(sent_0, CORE, size), hop(sent_1, CORE, size)
    steps = [((bit, bit), side[k] > 0) for k, bit in enumerate(top_bits(size))]
    steps.append((SUM, side[len(steps)] > 0))
    gathers = steps[-1:] + steps[:-1]
    first_hop = hop(row_master[None], gathers[0][0], size)
    master, other = row_copy[None], first_hop
    for k, (bits, upper) in enumerate(gathers):
        if k > 0:
            other = hop(master, bits, size)
        master = joined(master, other, upper).astype(jnp.bfloat16)
    mine = master.reshape(group_rows, width)
    beside = hop(mine, SPLIT, size)
    history, _ = lax.optimization_barrier((history[None], mine))
    for bits, upper in gathers[:-1]:
        history = joined(history, hop(history, bits, size), upper)

    def gradient_of(kind, rows, kept, received, *after):
        return pl.pallas_call(
            functools.partial(rows_kernel, chunk),
            out_shape=(pltpu.VMEM((group_rows, width), kind), pltpu.VMEM((group_rows, block_columns), jnp.bfloat16)),
            in_specs=[VMEM] * 6 + [ANY] * len(after),
            out_specs=[VMEM] * 2,
            compiler_params=PARAMS,
            cost_estimate=pl.CostEstimate(flops=8 * group_rows * block_columns * width, bytes_accessed=0, transcendentals=4 * group_rows * block_columns),
            name="rows",
        )(*[near(v) for v in (rows, kept, received, column_copy, other_columns, turned)], *after)

    part_late, slopes_1 = gradient_of(jnp.bfloat16, beside, kept_1, received_1)
    part_early, slopes_0 = gradient_of(jnp.float32, mine, kept_0, received_0, first_hop)
    own_rows, part_late = lax.optimization_barrier((jnp.concatenate([mine, beside]), part_late))
    others = hop(own_rows, CORE, size)
    others, history = lax.optimization_barrier((others, history))

    part = part_early + hop(part_late, SPLIT, size).astype(jnp.float32)
    struct = jax.ShapeDtypeStruct(column_master.shape, jnp.float32)
    new_columns, new_column_history = pl.pallas_call(
        functools.partial(columns_kernel, total_rows, chunk),
        out_shape=(struct, struct),
        in_specs=[VMEM] * 10,
        out_specs=[HBM] * 2,
        scratch_shapes=[
            pltpu.VMEM((2 * group_rows, block_columns), jnp.bfloat16),
            pltpu.VMEM(column_master.shape, jnp.float32),
            pltpu.VMEM(column_master.shape, jnp.float32),
            pltpu.SemaphoreType.DMA((2 * (block_columns // 128),)),
        ],
        compiler_params=PARAMS,
        cost_estimate=pl.CostEstimate(flops=2 * total_rows * block_columns * width, bytes_accessed=4 * column_master.size * 4, transcendentals=0),
        name="columns",
    )(*[near(v) for v in (column_master, column_history, turned, sent_0, sent_1, mine, beside, others, slopes_0, slopes_1)])

    last_history = hop(history, gathers[-1][0], size)
    for bits, upper in steps:
        rounded = part.astype(jnp.bfloat16)
        part = rounded.astype(jnp.float32) + hop(rounded, bits, size).astype(jnp.float32)
    history = joined(history, last_history, gathers[-1][1])

    def adagrad(master, history, gradient):
        updated = history + gradient * gradient
        return master - step_size * gradient * lax.rsqrt(updated), updated

    gradient = part.reshape(group, own, width) / all_columns
    own_gradient = lax.dynamic_index_in_dim(gradient, last_bit(me) * (group // 2) + (me >> 3), 0, keepdims=False)
    new_rows, new_row_history = adagrad(row_master, row_history, own_gradient)
    copy = adagrad(master.astype(jnp.float32), history.astype(jnp.float32), gradient)[0].astype(jnp.bfloat16)
    copy, new_columns = lax.optimization_barrier((copy, new_columns))
    beside = hop(copy, SPLIT, size)
    grid_rows = pl.pallas_call(
        place_kernel,
        out_shape=jax.ShapeDtypeStruct(grid + (width,), jnp.bfloat16),
        in_specs=[VMEM] * 4,
        out_specs=VMEM,
        compiler_params=PARAMS,
        name="place",
    )(near(copy), near(beside), near(hop(copy, CORE, size)), near(hop(beside, CORE, size)))
    return (grid_rows.reshape(total_rows, width), new_rows, new_row_history, new_columns, new_column_history)


def solution(mesh):
    return jax.shard_map(
        per_device,
        mesh=mesh,
        in_specs=(
            P("parts", "col"),
            P("parts"),
            P(("parts", "col")),
            P(("parts", "col"), None),
            P(("parts", "col"), None),
            P(("parts", "col"), None),
            P(("parts", "col"), None),
        ),
        out_specs=(
            P("parts", None),
            P(("parts", "col"), None),
            P(("parts", "col"), None),
            P(("parts", "col"), None),
            P(("parts", "col"), None),
        ),
        check_vma=False,
    )
```
